32 devices in a mesh: dp: 4 (over x, core), expert: 8 (over z, y).
Axes of the slice: x: 2, y: 2, z: 4, core: 2. Of those that a mesh axis runs over, the one named last changes fastest.
Arguments:
- tokens: bfloat16 [4096, 1024], P(('dp', 'expert')), may hold values from -6 to 6
- router: float32 [1024, 8], replicated, may hold values from -0.1875 to 0.1875
- expert_lists: int32 [4096, 4], P(('dp', 'expert')), may hold values from 0 to 7, as said below
- slot_positions: int32 [4096, 4], P(('dp', 'expert')), may hold values from 0 to 79, as said below
- teacher_gate: bfloat16 [1024, 2752], P(None, 'expert'), may hold values from -0.1875 to 0.1875
- teacher_up: bfloat16 [1024, 2752], P(None, 'expert'), may hold values from -0.1875 to 0.1875
- teacher_down: bfloat16 [2752, 1024], P('expert'), may hold values from -0.109375 to 0.109375
- expert_gate: bfloat16 [8, 1024, 704], P('expert'), may hold values from -0.1875 to 0.1875
- expert_up: bfloat16 [8, 1024, 704], P('expert'), may hold values from -0.1875 to 0.1875
- expert_down: bfloat16 [8, 704, 1024], P('expert'), may hold values from -0.21875 to 0.21875
Outputs:
- grad_gate: float32 [8, 1024, 704], P('expert', 'dp')
- grad_up: float32 [8, 1024, 704], P('expert', 'dp')
- grad_down: float32 [8, 704, 1024], P('expert', None, 'dp')
The draws below stay inside these ranges and needn't reach their ends.
Inputs may be any that keep to these rules, and one draw needn't show every extreme that they name: `expert_lists`: the k-th expert of every token lies among k * 2 to (k + 1) * 2 - 1. The tokens of one device name each expert at most 80 times. For each index of dp and each such quarter of the experts, one expert is named exactly 80 times by the tokens of every device of that index. `slot_positions`: copies from the tokens of one device that name the same expert have distinct slots.
All inputs are finite; a program needn't handle non-finite values.
Results may differ from the reference program's by a relative error of at most 0.015.
Values may be sent and summed in bfloat16 or wider, within the bound.
A program may use at most 128 MiB of HBM per device.

```python
import math
import jax
import jax.numpy as jnp
from jax import lax

D = 1024
EFF = 704
TFF = 2752
TOPK = 4
TOK_DEV = 128
EXPERTS = 8
CAP = 80
TOKENS = 4096
ROWS = 2048
N_DP = 4
N_EXPERT = 8


def route_tables(key):
    blocks = TOKENS // TOK_DEV
    quarter = EXPERTS // TOPK
    others = max(quarter - 1, 1)
    remain = TOK_DEV - CAP
    half_step = max(min(remain // (2 * others), (CAP - remain // others - 2) // 2), 0)
    hot_table = jax.random.randint(jax.random.fold_in(key, 7101), (N_DP, TOPK), 0, quarter)

    def one_column(block_index, column):
        column_key = jax.random.fold_in(jax.random.fold_in(key, 7202), block_index * TOPK + column)
        keys_three = jax.random.split(column_key, 3)
        order = jax.random.permutation(keys_three[0], TOK_DEV).astype(jnp.int32)
        inner = jnp.arange(1, others, dtype=jnp.int32)
        jitter = jax.random.randint(keys_three[1], (others - 1,), -half_step, half_step + 1)
        cuts = inner * remain // others + jitter
        rest = order - CAP
        label_rest = 1 + jnp.sum((rest[:, None] >= cuts[None, :]).astype(jnp.int32), axis=1)
        starts = jnp.concatenate([jnp.zeros((1,), jnp.int32), cuts.astype(jnp.int32)])
        rank_rest = rest - starts[label_rest - 1]
        is_hot = order < CAP
        label = jnp.where(is_hot, 0, label_rest)
        rank = jnp.where(is_hot, order, rank_rest)
        hot_here = hot_table[block_index // N_EXPERT, column]
        within = (label + hot_here) % quarter
        expert_id = column * quarter + within
        shifts = jax.random.randint(keys_three[2], (quarter,), 0, CAP)
        slot_id = (rank + shifts[within]) % CAP
        return (expert_id.astype(jnp.int32), slot_id.astype(jnp.int32))
    inner_map = jax.vmap(one_column, in_axes=(None, 0))
    outer_map = jax.vmap(inner_map, in_axes=(0, None))
    expert_ids, slot_ids = outer_map(jnp.arange(blocks, dtype=jnp.int32), jnp.arange(TOPK, dtype=jnp.int32))
    expert_ids = jnp.transpose(expert_ids, (0, 2, 1)).reshape(TOKENS, TOPK)
    slot_ids = jnp.transpose(slot_ids, (0, 2, 1)).reshape(TOKENS, TOPK)
    return (expert_ids, slot_ids)


def draw_expert_lists(key, part):
    return route_tables(key)[0]


def draw_slot_positions(key, part):
    return route_tables(key)[1]


def level_of(rng, extent, cuts, least, top_value):
    gain = 1.0
    for axis_at, blocks in cuts:
        heights = jax.random.uniform(jax.random.fold_in(jax.random.fold_in(rng, 6), axis_at), (blocks,), jnp.float32, least / len(cuts), top_value / len(cuts))
        gain = gain * jnp.repeat(jnp.exp(heights), extent[axis_at] // blocks).reshape((-1,) + (1,) * (len(extent) - 1 - axis_at))
    return gain


def centred(rng, dims, spread, reach, cuts=(), kind=jnp.bfloat16):
    array = spread * jax.random.normal(rng, dims, jnp.float32)
    if cuts:
        array = array * level_of(rng, dims, cuts, -0.22, 0.18)
    return jnp.clip(array, -reach, reach).astype(kind)


def setup_inputs(seed: int = 0) -> dict:
    seeds = jax.random.split(jax.random.key(seed), 11)
    tokens = centred(seeds[0], (TOKENS, D), 1.0, 6.0, ((0, 32),))
    router = centred(seeds[1], (D, EXPERTS), D ** -0.5, 0.1875, (), jnp.float32)
    expert_lists = draw_expert_lists(jax.random.fold_in(seeds[10], 71), 0)
    slot_positions = draw_slot_positions(jax.random.fold_in(seeds[10], 71), 0)
    teacher_gate = centred(seeds[4], (D, TFF), D ** -0.5, 0.1875, ((1, 8),))
    teacher_up = centred(seeds[5], (D, TFF), D ** -0.5, 0.1875, ((1, 8),))
    teacher_down = centred(seeds[6], (TFF, D), TFF ** -0.5, 0.109375, ((0, 8),))
    expert_gate = centred(seeds[7], (EXPERTS, D, EFF), D ** -0.5, 0.1875, ((0, 8),))
    expert_up = centred(seeds[8], (EXPERTS, D, EFF), D ** -0.5, 0.1875, ((0, 8),))
    expert_down = centred(seeds[9], (EXPERTS, EFF, D), EFF ** -0.5, 0.21875, ((0, 8),))
    return dict(tokens=tokens, router=router, expert_lists=expert_lists, slot_positions=slot_positions, teacher_gate=teacher_gate, teacher_up=teacher_up, teacher_down=teacher_down, expert_gate=expert_gate, expert_up=expert_up, expert_down=expert_down)


def silu_value(values):
    return values * jax.nn.sigmoid(values)

def reference(tokens, router, expert_lists, slot_positions, teacher_gate, teacher_up, teacher_down, expert_gate, expert_up, expert_down):
    shard_width = TFF // N_EXPERT

    def teacher_step(running, block_index):
        first_unit = (block_index * shard_width).astype(jnp.int32)
        gate_block = lax.dynamic_slice_in_dim(teacher_gate, first_unit, shard_width, 1)
        up_block = lax.dynamic_slice_in_dim(teacher_up, first_unit, shard_width, 1)
        down_block = lax.dynamic_slice_in_dim(teacher_down, first_unit, shard_width, 0)
        pre_a = jnp.dot(tokens, gate_block, preferred_element_type=jnp.float32)
        pre_b = jnp.dot(tokens, up_block, preferred_element_type=jnp.float32)
        hidden_block = (silu_value(pre_a) * pre_b).astype(jnp.bfloat16)
        partial_out = jnp.dot(hidden_block, down_block, preferred_element_type=jnp.float32).astype(jnp.bfloat16)
        partial_out = lax.optimization_barrier(partial_out)
        return (running + partial_out.astype(jnp.float32), None)
    teacher_total, unused = lax.scan(teacher_step, jnp.zeros((TOKENS, D), jnp.float32), jnp.arange(N_EXPERT, dtype=jnp.int32))
    target = teacher_total.astype(jnp.bfloat16)
    logits = jnp.dot(tokens.astype(jnp.float32), router, precision=lax.Precision.HIGHEST)
    picked = jnp.take_along_axis(logits, expert_lists, axis=1)
    sigmoid_pick = jax.nn.sigmoid(picked)
    weights = sigmoid_pick / lax.optimization_barrier(jnp.sum(sigmoid_pick, axis=1, keepdims=True))
    loss_scale = TOPK / math.sqrt(ROWS)
    group_size = TOK_DEV * N_EXPERT
    buffer_rows = N_EXPERT * CAP
    highest = lax.Precision.HIGHEST

    def group_step(carry, group_index):
        first_row = (group_index * group_size).astype(jnp.int32)
        group_tokens = lax.dynamic_slice_in_dim(tokens, first_row, group_size, 0)
        group_lists = lax.dynamic_slice_in_dim(expert_lists, first_row, group_size, 0)
        group_slots = lax.dynamic_slice_in_dim(slot_positions, first_row, group_size, 0)
        group_weights = lax.dynamic_slice_in_dim(weights, first_row, group_size, 0)
        group_target = lax.dynamic_slice_in_dim(target, first_row, group_size, 0)
        source = (jnp.arange(group_size, dtype=jnp.int32) // TOK_DEV)[:, None]
        flat_index = group_lists * buffer_rows + source * CAP + group_slots
        owner_index = jnp.zeros((EXPERTS * buffer_rows,), jnp.int32).at[flat_index.reshape(-1)].set(jnp.repeat(jnp.arange(group_size, dtype=jnp.int32) + 1, TOPK))
        filled = owner_index > 0
        expert_rows = jnp.where(filled[:, None], group_tokens[jnp.maximum(owner_index - 1, 0)], jnp.zeros((), jnp.bfloat16)).reshape(EXPERTS, buffer_rows, D)
        rows_wide = expert_rows.astype(jnp.float32)
        pre_gate = jnp.einsum('end,edf->enf', rows_wide, expert_gate.astype(jnp.float32), precision=highest)
        pre_up = jnp.einsum('end,edf->enf', rows_wide, expert_up.astype(jnp.float32), precision=highest)
        hidden = (silu_value(pre_gate) * pre_up).astype(jnp.bfloat16)
        down_wide = expert_down.astype(jnp.float32)
        expert_out = jnp.einsum('enf,efd->end', hidden.astype(jnp.float32), down_wide, precision=highest).astype(jnp.bfloat16)
        copies = expert_out.reshape(EXPERTS * buffer_rows, D)[flat_index]
        student = lax.optimization_barrier(jnp.sum(group_weights[:, :, None] * copies.astype(jnp.float32), axis=1))
        scaled_error = (student - group_target.astype(jnp.float32)) * loss_scale
        cotangent = (group_weights[:, :, None] * scaled_error[:, None, :]).astype(jnp.bfloat16)
        cot_buffer = jnp.zeros((EXPERTS * buffer_rows, D), jnp.bfloat16).at[flat_index.reshape(-1)].set(cotangent.reshape(-1, D)).reshape(EXPERTS, buffer_rows, D)
        cot_wide = cot_buffer.astype(jnp.float32)
        grad_hidden = jnp.einsum('end,efd->enf', cot_wide, down_wide, precision=highest)
        gate_sigmoid = jax.nn.sigmoid(pre_gate)
        grad_pre_gate = (grad_hidden * pre_up * gate_sigmoid * (1.0 + pre_gate * (1.0 - gate_sigmoid))).astype(jnp.bfloat16)
        grad_pre_up = (grad_hidden * (pre_gate * gate_sigmoid)).astype(jnp.bfloat16)
        part_gate = jnp.einsum('end,enf->edf', rows_wide, grad_pre_gate.astype(jnp.float32), precision=highest).astype(jnp.bfloat16)
        part_up = jnp.einsum('end,enf->edf', rows_wide, grad_pre_up.astype(jnp.float32), precision=highest).astype(jnp.bfloat16)
        part_down = jnp.einsum('enf,end->efd', hidden.astype(jnp.float32), cot_wide, precision=highest).astype(jnp.bfloat16)
        part_gate, part_up, part_down = lax.optimization_barrier((part_gate, part_up, part_down))
        sum_gate, sum_up, sum_down = carry
        return ((sum_gate + part_gate.astype(jnp.float32), sum_up + part_up.astype(jnp.float32), sum_down + part_down.astype(jnp.float32)), None)
    start_carry = (jnp.zeros((EXPERTS, D, EFF), jnp.float32), jnp.zeros((EXPERTS, D, EFF), jnp.float32), jnp.zeros((EXPERTS, EFF, D), jnp.float32))
    sums, unused_too = lax.scan(group_step, start_carry, jnp.arange(N_DP, dtype=jnp.int32))
    return (sums[0], sums[1], sums[2])
```

```python
import functools
import math

import jax
import jax.numpy as jnp
from jax import lax
from jax.experimental import pallas as pl
from jax.experimental.pallas import tpu as pltpu
from jax.sharding import PartitionSpec as P


def silu_value(values):
    return values * jax.nn.sigmoid(values)


def teacher_rows(row_block, teacher_gate, teacher_up, teacher_down):
    pre_a = jnp.dot(row_block, teacher_gate, preferred_element_type=jnp.float32)
    pre_b = jnp.dot(row_block, teacher_up, preferred_element_type=jnp.float32)
    hidden_block = (silu_value(pre_a) * pre_b).astype(jnp.bfloat16)
    return jnp.dot(hidden_block, teacher_down, preferred_element_type=jnp.float32)


def make_term(group_tokens, teacher_gate, teacher_up, teacher_down):

    def teacher_term(first_row, row_count):
        return teacher_rows(group_tokens, teacher_gate, teacher_up, teacher_down)

    return teacher_term


def expert_forward(expert_rows, expert_gate, expert_up, expert_down):
    pre_gate = jnp.dot(expert_rows, expert_gate[0], preferred_element_type=jnp.float32)
    pre_up = jnp.dot(expert_rows, expert_up[0], preferred_element_type=jnp.float32)
    hidden = (silu_value(pre_gate) * pre_up).astype(jnp.bfloat16)
    output = jnp.dot(hidden, expert_down[0], preferred_element_type=jnp.float32).astype(
        jnp.bfloat16
    )
    return (pre_gate, pre_up, hidden, output)


def send_back(output_blocks):
    return lax.all_to_all(output_blocks, "expert", split_axis=0, concat_axis=0, tiled=True)


def on_device(
    tokens,
    router,
    expert_lists,
    slot_positions,
    teacher_gate,
    teacher_up,
    teacher_down,
    expert_gate,
    expert_up,
    expert_down,
):
    tok_count, model_width = tokens.shape
    top_count = expert_lists.shape[1]
    experts = router.shape[1]
    expert_devices = lax.axis_size("expert")
    data_devices = lax.axis_size("dp")
    capacity = 5 * tok_count // experts
    loss_scale = top_count / math.sqrt(
        tok_count * data_devices * expert_devices * top_count / experts
    )
    logits = jnp.dot(tokens.astype(jnp.float32), router, precision=lax.Precision.HIGHEST)
    chosen_mask = expert_lists[:, :, None] == jnp.arange(experts, dtype=jnp.int32)[None, None, :]
    picked = jnp.sum(jnp.where(chosen_mask, logits[:, None, :], 0.0), axis=2)
    sigmoid_pick = jax.nn.sigmoid(picked)
    weights = sigmoid_pick / jnp.sum(sigmoid_pick, axis=1, keepdims=True)
    position = expert_lists * capacity + slot_positions
    entry_index = (
        jnp.zeros((experts * capacity,), jnp.int32)
        .at[position.reshape(-1)]
        .set(jnp.arange(tok_count * top_count, dtype=jnp.int32) + 1)
    )
    filled = entry_index > 0
    entry_row = jnp.maximum(entry_index - 1, 0)
    group_tokens = lax.all_gather(tokens, "expert", axis=0, tiled=True)
    teacher_term = make_term(group_tokens, teacher_gate, teacher_up, teacher_down)
    target = lax.psum_scatter(
        teacher_term(jnp.int32(0), lax.axis_size("expert") * tok_count).astype(jnp.bfloat16),
        "expert",
        scatter_dimension=0,
        tiled=True,
    )
    lists_group, slots_group = (
        lax.all_gather(expert_lists, "expert", axis=0, tiled=True),
        lax.all_gather(slot_positions, "expert", axis=0, tiled=True),
    )
    my_expert = lax.axis_index("expert")
    group_count = lists_group.shape[0]
    source = (jnp.arange(group_count, dtype=jnp.int32) // tok_count)[:, None]
    local_slot = jnp.where(
        lists_group == my_expert, source * capacity + slots_group, expert_devices * capacity
    )
    owner_index = (
        jnp.zeros((expert_devices * capacity,), jnp.int32)
        .at[local_slot.reshape(-1)]
        .set(jnp.repeat(jnp.arange(group_count, dtype=jnp.int32) + 1, top_count), mode="drop")
    )
    expert_rows = jnp.where(
        (owner_index > 0)[:, None],
        group_tokens[jnp.maximum(owner_index - 1, 0)],
        jnp.zeros((), jnp.bfloat16),
    )
    pre_gate, pre_up, hidden, output = expert_forward(
        expert_rows, expert_gate, expert_up, expert_down
    )
    returned = send_back(output.reshape(expert_devices, capacity, model_width))
    flat_back = returned.reshape(experts * capacity, model_width)
    copies = flat_back[position]
    student = jnp.sum(weights[:, :, None] * copies.astype(jnp.float32), axis=1)
    scaled_error = (student - target.astype(jnp.float32)) * loss_scale
    cotangent = (
        (weights[:, :, None] * scaled_error[:, None, :])
        .astype(jnp.bfloat16)
        .reshape(tok_count * top_count, model_width)
    )
    cot_send = jnp.where(
        filled[:, None], cotangent[entry_row], jnp.zeros((), jnp.bfloat16)
    ).reshape(experts, capacity, model_width)
    cot_recv = lax.all_to_all(cot_send, "expert", split_axis=0, concat_axis=0, tiled=True).reshape(
        -1, model_width
    )
    grad_hidden = lax.dot_general(
        cot_recv, expert_down[0], (((1,), (1,)), ((), ())), preferred_element_type=jnp.float32
    )
    gate_sigmoid = jax.nn.sigmoid(pre_gate)
    grad_pre_gate = (
        grad_hidden * pre_up * gate_sigmoid * (1.0 + pre_gate * (1.0 - gate_sigmoid))
    ).astype(jnp.bfloat16)
    grad_pre_up = (grad_hidden * (pre_gate * gate_sigmoid)).astype(jnp.bfloat16)
    part_down = lax.dot_general(
        hidden, cot_recv, (((0,), (0,)), ((), ())), preferred_element_type=jnp.float32
    )
    part_gate = lax.dot_general(
        expert_rows, grad_pre_gate, (((0,), (0,)), ((), ())), preferred_element_type=jnp.float32
    )
    part_up = lax.dot_general(
        expert_rows, grad_pre_up, (((0,), (0,)), ((), ())), preferred_element_type=jnp.float32
    )
    sum_gate, sum_up = (
        lax.psum_scatter(
            part_gate.astype(jnp.bfloat16), "dp", scatter_dimension=0, tiled=True
        ).astype(jnp.float32),
        lax.psum_scatter(
            part_up.astype(jnp.bfloat16), "dp", scatter_dimension=0, tiled=True
        ).astype(jnp.float32),
    )
    sum_down = lax.psum_scatter(
        part_down.astype(jnp.bfloat16), "dp", scatter_dimension=1, tiled=True
    ).astype(jnp.float32)
    return (sum_gate[None], sum_up[None], sum_down[None])


PAIR = 2
BF16 = jnp.bfloat16
F32 = jnp.float32


def near_first(count):
    return [sorted(range(count), key=lambda d, z=z: (abs(d - z), d < z if 2 * z < count else d > z)) for z in range(count)]


def fused_kernel(
    line,
    data_devices,
    loss_scale,
    tokens_ref,
    router_ref,
    lists_ref,
    tgate_hbm,
    tup_hbm,
    tdown_hbm,
    gate_hbm,
    up_hbm,
    down_hbm,
    out_gate,
    out_up,
    out_down,
    tgate,
    tup,
    tdown,
    egate,
    eup,
    edown,
    rows_buf,
    err_buf,
    w_buf,
    pre_gate,
    pre_up,
    hidden,
    grad_pre_gate,
    grad_pre_up,
    cot,
    part_own,
    y_send,
    y_recv,
    z_send,
    z_recv,
    core_send,
    core_recv,
    core_send_d,
    core_recv_d,
    keep,
    keep_d,
    x_send,
    x_recv,
    x_send_d,
    x_recv_d,
    load_sem,
    w_ssem,
    w_rsem,
    ag_rsem,
    ag_ysem,
    ag_zsem,
    rs_ysem,
    rs_yrsem,
    rs_zsem,
    rs_zrsem,
    c_ssem,
    c_rsem,
    x_ssem,
    x_rsem,
):
    tok_count, width = tokens_ref.shape
    experts = router_ref.shape[1]
    dp = lax.axis_index("dp")
    me = lax.axis_index("expert")
    z = me // PAIR
    y = me % PAIR
    peers = line * PAIR
    pair_rows = PAIR * tok_count
    y_peer = (dp, me + 1 - 2 * y)
    x_at = dp // PAIR
    core = dp % PAIR
    core_peer = (dp + 1 - 2 * core, me)
    x_peer = (dp + PAIR - 2 * PAIR * x_at, me)
    table = near_first(line)

    def order(step):
        value = jnp.int32(0)
        for at in range(line):
            value = jnp.where(z == at, table[at][step], value)
        return value

    def remote(src, dst, ssem, rsem, device):
        return pltpu.make_async_remote_copy(
            src_ref=src,
            dst_ref=dst,
            send_sem=ssem,
            recv_sem=rsem,
            device_id=device,
            device_id_type=pl.DeviceIdType.MESH,
        )

    barrier = pltpu.get_barrier_semaphore()
    for step in range(1, peers):
        pl.semaphore_signal(
            barrier,
            inc=1,
            device_id=(dp, (me + step) % peers),
            device_id_type=pl.DeviceIdType.MESH,
        )
    for device in (core_peer, x_peer):
        pl.semaphore_signal(
            barrier, inc=1, device_id=device, device_id_type=pl.DeviceIdType.MESH
        )
    loads = [
        pltpu.make_async_copy(src, dst, load_sem.at[at])
        for at, (src, dst) in enumerate(
            (
                (tgate_hbm, tgate),
                (tup_hbm, tup),
                (tdown_hbm, tdown),
                (gate_hbm.at[0], egate),
                (up_hbm.at[0], eup),
                (down_hbm.at[0], edown),
            )
        )
    ]
    for load in loads:
        load.start()

    def block_of(buf, block):
        return buf.at[pl.ds(pl.multiple_of(block * tok_count, tok_count), tok_count)]

    block_of(rows_buf, me)[...] = tokens_ref[...]
    pl.semaphore_wait(barrier, peers - 1 + 2)

    def gather_start(buf, turn):
        mine = block_of(buf, me)

        @pl.when(z < line - 1)
        def _():
            remote(mine, mine, ag_zsem.at[turn, z], ag_rsem.at[turn, me], (dp, me + PAIR)).start()

        @pl.when(z > 0)
        def _():
            remote(mine, mine, ag_zsem.at[turn, line], ag_rsem.at[turn, me], (dp, me - PAIR)).start()

        remote(mine, mine, ag_ysem.at[turn, z], ag_rsem.at[turn, me], y_peer).start()

    def away(d):
        onward = jnp.where(d < z, z < line - 1, z > 0)
        return onward, (dp, jnp.where(d < z, me + PAIR, me - PAIR))

    def gather_rest(buf, turn, work):
        def recv(block):
            at = block_of(buf, block)
            remote(at, at, ag_ysem.at[turn, 0], ag_rsem.at[turn, block], y_peer).wait_recv()

        for step in range(1, line + 1):
            if step < line:
                d = order(step)
                block = d * PAIR + y
                recv(block)
                at = block_of(buf, block)
                onward, device = away(d)

                @pl.when(onward)
                def _():
                    remote(
                        at, at, ag_zsem.at[turn, d], ag_rsem.at[turn, block], device
                    ).start()

                remote(at, at, ag_ysem.at[turn, d], ag_rsem.at[turn, block], y_peer).start()
            before = order(step - 1)
            recv(before * PAIR + 1 - y)
            work(before)

    def gather_drain(buf, turn):
        mine = block_of(buf, me)

        @pl.when(z < line - 1)
        def _():
            remote(mine, mine, ag_zsem.at[turn, z], ag_rsem.at[turn, me], (dp, me + PAIR)).wait_send()

        @pl.when(z > 0)
        def _():
            remote(mine, mine, ag_zsem.at[turn, line], ag_rsem.at[turn, me], (dp, me - PAIR)).wait_send()

        for step in range(line):
            d = order(step)
            block = d * PAIR + y
            at = block_of(buf, block)
            if step:
                onward, device = away(d)

                @pl.when(onward)
                def _():
                    remote(
                        at, at, ag_zsem.at[turn, d], ag_rsem.at[turn, block], device
                    ).wait_send()

            remote(at, at, ag_ysem.at[turn, d], ag_rsem.at[turn, block], y_peer).wait_send()

    gather_start(rows_buf, 0)

    logits = jnp.dot(
        tokens_ref[...].astype(F32),
        router_ref[...],
        precision=lax.Precision.HIGHEST,
        preferred_element_type=F32,
    )
    expert_ids = lax.broadcasted_iota(jnp.int32, (tok_count, experts), 1)
    lists = lists_ref[...]
    chosen = lists[:, 0:1] == expert_ids
    for k in range(1, lists.shape[1]):
        chosen = jnp.logical_or(chosen, lists[:, k : k + 1] == expert_ids)
    picked = jnp.where(chosen, jax.nn.sigmoid(logits), 0.0)
    weights = picked / jnp.sum(picked, axis=1, keepdims=True)
    w_buf[me] = weights.T
    w_copies = []
    for step in range(1, peers):
        copy = remote(
            w_buf.at[me],
            w_buf.at[me],
            w_ssem.at[step - 1],
            w_rsem.at[step - 1],
            (dp, (me + step) % peers),
        )
        copy.start()
        w_copies.append(copy)
    for load in loads:
        load.wait()
    for copy in w_copies:
        copy.wait()

    def pair_weights(d):
        columns = []
        for part in range(PAIR):
            table_part = w_buf[d * PAIR + part].T
            columns.append(
                jnp.sum(jnp.where(expert_ids == me, table_part, 0.0), axis=1, keepdims=True)
            )
        return jnp.concatenate(columns, axis=0)

    def pair_of(d):
        return pl.ds(pl.multiple_of(d * pair_rows, pair_rows), pair_rows)

    def y_copy(d):
        return remote(
            y_send.at[d], y_recv.at[d], rs_ysem.at[d], rs_yrsem.at[d], y_peer
        )

    def forward(d):
        where = pair_of(d)
        rows = rows_buf[where, :]
        pre_a = jnp.dot(rows, tgate[...], preferred_element_type=F32)
        pre_b = jnp.dot(rows, tup[...], preferred_element_type=F32)
        teacher_hidden = (silu_value(pre_a) * pre_b).astype(BF16)
        teacher = jnp.dot(teacher_hidden, tdown[...], preferred_element_type=F32)
        gate_values = jnp.dot(rows, egate[...], preferred_element_type=F32)
        up_values = jnp.dot(rows, eup[...], preferred_element_type=F32)
        pre_gate[where, :] = gate_values
        pre_up[where, :] = up_values
        hidden_values = (silu_value(gate_values) * up_values).astype(BF16)
        hidden[where, :] = hidden_values
        output = jnp.dot(hidden_values, edown[...], preferred_element_type=F32)
        partial = pair_weights(d) * output - teacher
        low = partial[:tok_count]
        high = partial[tok_count:]
        part_own[d] = jnp.where(y == 0, low, high)
        y_send[d] = jnp.where(y == 0, high, low).astype(BF16)
        y_copy(d).start()

    gather_rest(rows_buf, 0, forward)

    def z_copy(d):
        rising = d > z
        way = jnp.where(rising, 0, 1)
        return remote(
            z_send.at[d],
            z_recv.at[way, d],
            rs_zsem.at[d],
            rs_zrsem.at[way, d],
            (dp, jnp.where(rising, me + PAIR, me - PAIR)),
        )

    def z_arrived(way, d):
        remote(
            z_send.at[d], z_recv.at[way, d], rs_zsem.at[d], rs_zrsem.at[way, d], y_peer
        ).wait_recv()
        part_own[d] += z_recv[way, d].astype(F32)

    for step in range(line - 1, -1, -1):
        d = order(step)
        y_copy(d).wait_recv()
        part_own[d] += y_recv[d].astype(F32)

        @pl.when(jnp.logical_and(d >= z, z > 0))
        def _():
            z_arrived(0, d)

        @pl.when(jnp.logical_and(d <= z, z < line - 1))
        def _():
            z_arrived(1, d)

        if step:
            z_send[d] = part_own[d].astype(BF16)
            z_copy(d).start()
        else:
            block_of(err_buf, me)[...] = (part_own[d] * loss_scale).astype(BF16)

    gather_start(err_buf, 1)
    gather_drain(rows_buf, 0)
    for step in range(line):
        d = order(step)
        y_copy(d).wait_send()
        if step:
            z_copy(d).wait_send()

    def backward(d):
        where = pair_of(d)
        cot_values = (pair_weights(d) * err_buf[where, :].astype(F32)).astype(BF16)
        cot[where, :] = cot_values
        grad_hidden = lax.dot_general(
            cot_values, edown[...], (((1,), (1,)), ((), ())), preferred_element_type=F32
        )
        gate_values = pre_gate[where, :]
        gate_sigmoid = jax.nn.sigmoid(gate_values)
        grad_pre_gate[where, :] = (
            grad_hidden
            * pre_up[where, :]
            * gate_sigmoid
            * (1.0 + gate_values * (1.0 - gate_sigmoid))
        ).astype(BF16)
        grad_pre_up[where, :] = (grad_hidden * (gate_values * gate_sigmoid)).astype(BF16)

    gather_rest(err_buf, 1, backward)

    quarter = width // data_devices
    contract = (((0,), (0,)), ((), ()))

    def part(which, q):
        columns = pl.ds(pl.multiple_of(q * quarter, quarter), quarter)
        if which == 2:
            return lax.dot_general(
                hidden[...], cot[:, columns], contract, preferred_element_type=F32
            )
        grads = grad_pre_gate if which == 0 else grad_pre_up
        return lax.dot_general(
            rows_buf[:, columns], grads[...], contract, preferred_element_type=F32
        )

    def at_part(which, wide, tall):
        return tall if which == 2 else wide.at[which]

    def core_copy(which, slot):
        return remote(
            at_part(which, core_send, core_send_d).at[slot],
            at_part(which, core_recv, core_recv_d).at[slot],
            c_ssem.at[which, slot],
            c_rsem.at[which, slot],
            core_peer,
        )

    def x_copy(which):
        return remote(
            at_part(which, x_send, x_send_d),
            at_part(which, x_recv, x_recv_d),
            x_ssem.at[which],
            x_rsem.at[which],
            x_peer,
        )

    x_of = (1 - x_at, x_at)
    for which in (0, 1, 2):
        held = at_part(which, keep, keep_d)
        sends = at_part(which, core_send, core_send_d)
        recvs = at_part(which, core_recv, core_recv_d)
        for slot in range(PAIR):
            sends[slot] = part(which, x_of[slot] * PAIR + 1 - core).astype(BF16)
            core_copy(which, slot).start()
            own = part(which, x_of[slot] * PAIR + core)
            core_copy(which, slot).wait_recv()
            total = own + recvs[slot].astype(F32)
            if slot == 0:
                at_part(which, x_send, x_send_d)[...] = total.astype(BF16)
                x_copy(which).start()
            else:
                held[...] = total
    outs = (out_gate, out_up, out_down)
    for which in (0, 1, 2):
        x_copy(which).wait_recv()
        outs[which][0] = (
            at_part(which, keep, keep_d)[...] + at_part(which, x_recv, x_recv_d)[...].astype(F32)
        )
    gather_drain(err_buf, 1)
    for which in (0, 1, 2):
        x_copy(which).wait_send()
        for slot in range(PAIR):
            core_copy(which, slot).wait_send()


def fused_on_device(
    tokens,
    router,
    expert_lists,
    slot_positions,
    teacher_gate,
    teacher_up,
    teacher_down,
    expert_gate,
    expert_up,
    expert_down,
):
    tok_count, width = tokens.shape
    experts = router.shape[1]
    top_count = expert_lists.shape[1]
    peers = lax.axis_size("expert")
    data_devices = lax.axis_size("dp")
    line = peers // PAIR
    units = expert_gate.shape[2]
    group = peers * tok_count
    quarter = width // data_devices
    loss_scale = top_count / math.sqrt(group * data_devices * top_count / experts)
    vmem = pl.BlockSpec(memory_space=pltpu.VMEM)
    hbm = pl.BlockSpec(memory_space=pl.ANY)
    flops = 2 * group * width * (3 * teacher_gate.shape[1] + 7 * units)
    wide = (quarter, units)
    tall = (units, quarter)
    dma = pltpu.SemaphoreType.DMA
    return pl.pallas_call(
        functools.partial(fused_kernel, line, data_devices, loss_scale),
        out_shape=(
            jax.ShapeDtypeStruct((1,) + wide, F32),
            jax.ShapeDtypeStruct((1,) + wide, F32),
            jax.ShapeDtypeStruct((1,) + tall, F32),
        ),
        in_specs=[vmem] * 3 + [hbm] * 6,
        out_specs=(vmem, vmem, vmem),
        scratch_shapes=[
            pltpu.VMEM(teacher_gate.shape, BF16),
            pltpu.VMEM(teacher_up.shape, BF16),
            pltpu.VMEM(teacher_down.shape, BF16),
            pltpu.VMEM(expert_gate.shape[1:], BF16),
            pltpu.VMEM(expert_up.shape[1:], BF16),
            pltpu.VMEM(expert_down.shape[1:], BF16),
            pltpu.VMEM((group, width), BF16),
            pltpu.VMEM((group, width), BF16),
            pltpu.VMEM((peers, experts, tok_count), F32),
            pltpu.VMEM((group, units), F32),
            pltpu.VMEM((group, units), F32),
            pltpu.VMEM((group, units), BF16),
            pltpu.VMEM((group, units), BF16),
            pltpu.VMEM((group, units), BF16),
            pltpu.VMEM((group, width), BF16),
            pltpu.VMEM((line, tok_count, width), F32),
            pltpu.VMEM((line, tok_count, width), BF16),
            pltpu.VMEM((line, tok_count, width), BF16),
            pltpu.VMEM((line, tok_count, width), BF16),
            pltpu.VMEM((2, line, tok_count, width), BF16),
            pltpu.VMEM((2, PAIR) + wide, BF16),
            pltpu.VMEM((2, PAIR) + wide, BF16),
            pltpu.VMEM((PAIR,) + tall, BF16),
            pltpu.VMEM((PAIR,) + tall, BF16),
            pltpu.VMEM((2,) + wide, F32),
            pltpu.VMEM(tall, F32),
            pltpu.VMEM((2,) + wide, BF16),
            pltpu.VMEM((2,) + wide, BF16),
            pltpu.VMEM(tall, BF16),
            pltpu.VMEM(tall, BF16),
            dma((6,)),
            dma((peers - 1,)),
            dma((peers - 1,)),
            dma((2, peers)),
            dma((2, line)),
            dma((2, line + 1)),
            dma((line,)),
            dma((line,)),
            dma((line,)),
            dma((2, line)),
            dma((3, PAIR)),
            dma((3, PAIR)),
            dma((3,)),
            dma((3,)),
        ],
        compiler_params=pltpu.CompilerParams(
            collective_id=0, has_side_effects=True, vmem_limit_bytes=58 * 1024 * 1024
        ),
        cost_estimate=pl.CostEstimate(
            flops=flops, bytes_accessed=8 * width * units, transcendentals=2 * group * units
        ),
    )(
        tokens,
        router,
        expert_lists,
        teacher_gate,
        teacher_up,
        teacher_down,
        expert_gate,
        expert_up,
        expert_down,
    )


def fits_kernel(mesh):
    return mesh.shape["dp"] == PAIR * PAIR and mesh.shape["expert"] <= 4 * PAIR


def solution(mesh):
    return jax.shard_map(
        fused_on_device if fits_kernel(mesh) else on_device,
        mesh=mesh,
        in_specs=(
            P(("dp", "expert"), None),
            P(),
            P(("dp", "expert"), None),
            P(("dp", "expert"), None),
            P(None, "expert"),
            P(None, "expert"),
            P("expert", None),
            P("expert", None, None),
            P("expert", None, None),
            P("expert", None, None),
        ),
        out_specs=(P("expert", "dp", None), P("expert", "dp", None), P("expert", None, "dp")),
        check_vma=False,
    )
```

```python
import functools
import math

import jax
import jax.numpy as jnp
from jax import lax
from jax.experimental import pallas as pl
from jax.experimental.pallas import tpu as pltpu
from jax.sharding import PartitionSpec as P


def silu_value(values):
    return values * jax.nn.sigmoid(values)


def teacher_rows(row_block, teacher_gate, teacher_up, teacher_down):
    pre_a = jnp.dot(row_block, teacher_gate, preferred_element_type=jnp.float32)
    pre_b = jnp.dot(row_block, teacher_up, preferred_element_type=jnp.float32)
    hidden_block = (silu_value(pre_a) * pre_b).astype(jnp.bfloat16)
    return jnp.dot(hidden_block, teacher_down, preferred_element_type=jnp.float32)


def make_term(group_tokens, teacher_gate, teacher_up, teacher_down):

    def teacher_term(first_row, row_count):
        return teacher_rows(group_tokens, teacher_gate, teacher_up, teacher_down)

    return teacher_term


def expert_forward(expert_rows, expert_gate, expert_up, expert_down):
    pre_gate = jnp.dot(expert_rows, expert_gate[0], preferred_element_type=jnp.float32)
    pre_up = jnp.dot(expert_rows, expert_up[0], preferred_element_type=jnp.float32)
    hidden = (silu_value(pre_gate) * pre_up).astype(jnp.bfloat16)
    output = jnp.dot(hidden, expert_down[0], preferred_element_type=jnp.float32).astype(
        jnp.bfloat16
    )
    return (pre_gate, pre_up, hidden, output)


def send_back(output_blocks):
    return lax.all_to_all(output_blocks, "expert", split_axis=0, concat_axis=0, tiled=True)


def on_device(
    tokens,
    router,
    expert_lists,
    slot_positions,
    teacher_gate,
    teacher_up,
    teacher_down,
    expert_gate,
    expert_up,
    expert_down,
):
    tok_count, model_width = tokens.shape
    top_count = expert_lists.shape[1]
    experts = router.shape[1]
    expert_devices = lax.axis_size("expert")
    data_devices = lax.axis_size("dp")
    capacity = 5 * tok_count // experts
    loss_scale = top_count / math.sqrt(
        tok_count * data_devices * expert_devices * top_count / experts
    )
    logits = jnp.dot(tokens.astype(jnp.float32), router, precision=lax.Precision.HIGHEST)
    chosen_mask = expert_lists[:, :, None] == jnp.arange(experts, dtype=jnp.int32)[None, None, :]
    picked = jnp.sum(jnp.where(chosen_mask, logits[:, None, :], 0.0), axis=2)
    sigmoid_pick = jax.nn.sigmoid(picked)
    weights = sigmoid_pick / jnp.sum(sigmoid_pick, axis=1, keepdims=True)
    position = expert_lists * capacity + slot_positions
    entry_index = (
        jnp.zeros((experts * capacity,), jnp.int32)
        .at[position.reshape(-1)]
        .set(jnp.arange(tok_count * top_count, dtype=jnp.int32) + 1)
    )
    filled = entry_index > 0
    entry_row = jnp.maximum(entry_index - 1, 0)
    group_tokens = lax.all_gather(tokens, "expert", axis=0, tiled=True)
    teacher_term = make_term(group_tokens, teacher_gate, teacher_up, teacher_down)
    target = lax.psum_scatter(
        teacher_term(jnp.int32(0), lax.axis_size("expert") * tok_count).astype(jnp.bfloat16),
        "expert",
        scatter_dimension=0,
        tiled=True,
    )
    lists_group, slots_group = (
        lax.all_gather(expert_lists, "expert", axis=0, tiled=True),
        lax.all_gather(slot_positions, "expert", axis=0, tiled=True),
    )
    my_expert = lax.axis_index("expert")
    group_count = lists_group.shape[0]
    source = (jnp.arange(group_count, dtype=jnp.int32) // tok_count)[:, None]
    local_slot = jnp.where(
        lists_group == my_expert, source * capacity + slots_group, expert_devices * capacity
    )
    owner_index = (
        jnp.zeros((expert_devices * capacity,), jnp.int32)
        .at[local_slot.reshape(-1)]
        .set(jnp.repeat(jnp.arange(group_count, dtype=jnp.int32) + 1, top_count), mode="drop")
    )
    expert_rows = jnp.where(
        (owner_index > 0)[:, None],
        group_tokens[jnp.maximum(owner_index - 1, 0)],
        jnp.zeros((), jnp.bfloat16),
    )
    pre_gate, pre_up, hidden, output = expert_forward(
        expert_rows, expert_gate, expert_up, expert_down
    )
    returned = send_back(output.reshape(expert_devices, capacity, model_width))
    flat_back = returned.reshape(experts * capacity, model_width)
    copies = flat_back[position]
    student = jnp.sum(weights[:, :, None] * copies.astype(jnp.float32), axis=1)
    scaled_error = (student - target.astype(jnp.float32)) * loss_scale
    cotangent = (
        (weights[:, :, None] * scaled_error[:, None, :])
        .astype(jnp.bfloat16)
        .reshape(tok_count * top_count, model_width)
    )
    cot_send = jnp.where(
        filled[:, None], cotangent[entry_row], jnp.zeros((), jnp.bfloat16)
    ).reshape(experts, capacity, model_width)
    cot_recv = lax.all_to_all(cot_send, "expert", split_axis=0, concat_axis=0, tiled=True).reshape(
        -1, model_width
    )
    grad_hidden = lax.dot_general(
        cot_recv, expert_down[0], (((1,), (1,)), ((), ())), preferred_element_type=jnp.float32
    )
    gate_sigmoid = jax.nn.sigmoid(pre_gate)
    grad_pre_gate = (
        grad_hidden * pre_up * gate_sigmoid * (1.0 + pre_gate * (1.0 - gate_sigmoid))
    ).astype(jnp.bfloat16)
    grad_pre_up = (grad_hidden * (pre_gate * gate_sigmoid)).astype(jnp.bfloat16)
    part_down = lax.dot_general(
        hidden, cot_recv, (((0,), (0,)), ((), ())), preferred_element_type=jnp.float32
    )
    part_gate = lax.dot_general(
        expert_rows, grad_pre_gate, (((0,), (0,)), ((), ())), preferred_element_type=jnp.float32
    )
    part_up = lax.dot_general(
        expert_rows, grad_pre_up, (((0,), (0,)), ((), ())), preferred_element_type=jnp.float32
    )
    sum_gate, sum_up = (
        lax.psum_scatter(
            part_gate.astype(jnp.bfloat16), "dp", scatter_dimension=0, tiled=True
        ).astype(jnp.float32),
        lax.psum_scatter(
            part_up.astype(jnp.bfloat16), "dp", scatter_dimension=0, tiled=True
        ).astype(jnp.float32),
    )
    sum_down = lax.psum_scatter(
        part_down.astype(jnp.bfloat16), "dp", scatter_dimension=1, tiled=True
    ).astype(jnp.float32)
    return (sum_gate[None], sum_up[None], sum_down[None])


PAIR = 2
ROW_BY_ROW = (((1,), (1,)), ((), ()))
BF16 = jnp.bfloat16
F32 = jnp.float32


def near_first(count):
    return [sorted(range(count), key=lambda d, z=z: (abs(d - z), d < z if 2 * z < count else d > z)) for z in range(count)]


def fused_kernel(
    line,
    data_devices,
    loss_scale,
    tokens_ref,
    router_ref,
    lists_ref,
    tgate_hbm,
    tup_hbm,
    tdown_hbm,
    gate_hbm,
    up_hbm,
    down_hbm,
    out_gate,
    out_up,
    out_down,
    tgate,
    tup,
    tdown,
    egate,
    eup,
    edown,
    tdown_turned,
    edown_turned,
    rows_buf,
    err_buf,
    w_buf,
    pre_gate,
    pre_up,
    hidden,
    grad_pre_gate,
    grad_pre_up,
    cot,
    part_own,
    y_send,
    y_recv,
    z_send,
    z_recv,
    core_send,
    core_recv,
    keep,
    x_send,
    x_recv,
    load_sem,
    w_ssem,
    w_rsem,
    ag_rsem,
    ag_ysem,
    ag_zsem,
    rs_ysem,
    rs_yrsem,
    rs_zsem,
    rs_zrsem,
    c_ssem,
    c_rsem,
    x_ssem,
    x_rsem,
):
    tok_count, width = tokens_ref.shape
    experts = router_ref.shape[0]
    dp = lax.axis_index("dp")
    me = lax.axis_index("expert")
    z = me // PAIR
    y = me % PAIR
    peers = line * PAIR
    pair_rows = PAIR * tok_count
    y_peer = (dp, me + 1 - 2 * y)
    x_at = dp // PAIR
    core = dp % PAIR
    core_peer = (dp + 1 - 2 * core, me)
    x_peer = (dp + PAIR - 2 * PAIR * x_at, me)
    table = near_first(line)

    def order(step):
        value = jnp.int32(0)
        for at in range(line):
            value = jnp.where(z == at, table[at][step], value)
        return value

    def remote(src, dst, ssem, rsem, device):
        return pltpu.make_async_remote_copy(
            src_ref=src,
            dst_ref=dst,
            send_sem=ssem,
            recv_sem=rsem,
            device_id=device,
            device_id_type=pl.DeviceIdType.MESH,
        )

    barrier = pltpu.get_barrier_semaphore()
    for step in range(1, peers):
        pl.semaphore_signal(
            barrier,
            inc=1,
            device_id=(dp, (me + step) % peers),
            device_id_type=pl.DeviceIdType.MESH,
        )
    for device in (core_peer, x_peer):
        pl.semaphore_signal(
            barrier, inc=1, device_id=device, device_id_type=pl.DeviceIdType.MESH
        )
    loads = [
        pltpu.make_async_copy(src, dst, load_sem.at[at])
        for at, (src, dst) in enumerate(
            (
                (tgate_hbm, tgate),
                (tup_hbm, tup),
                (tdown_hbm, tdown),
                (gate_hbm.at[0], egate),
                (up_hbm.at[0], eup),
                (down_hbm.at[0], edown),
            )
        )
    ]
    for load in loads:
        load.start()

    def block_of(buf, block):
        if len(buf.shape) == 3:
            return buf.at[block]
        return buf.at[pl.ds(pl.multiple_of(block * tok_count, tok_count), tok_count)]

    block_of(rows_buf, me)[...] = tokens_ref[...]
    pl.semaphore_wait(barrier, peers - 1 + 2)

    def gather_start(buf, turn):
        mine = block_of(buf, me)

        @pl.when(z < line - 1)
        def _():
            remote(mine, mine, ag_zsem.at[turn, z], ag_rsem.at[turn, me], (dp, me + PAIR)).start()

        @pl.when(z > 0)
        def _():
            remote(mine, mine, ag_zsem.at[turn, line], ag_rsem.at[turn, me], (dp, me - PAIR)).start()

        remote(mine, mine, ag_ysem.at[turn, z], ag_rsem.at[turn, me], y_peer).start()

    def away(d):
        onward = jnp.where(d < z, z < line - 1, z > 0)
        return onward, (dp, jnp.where(d < z, me + PAIR, me - PAIR))

    def gather_rest(buf, turn, work):
        def recv(block):
            at = block_of(buf, block)
            remote(at, at, ag_ysem.at[turn, 0], ag_rsem.at[turn, block], y_peer).wait_recv()

        for step in range(1, line + 1):
            if step < line:
                d = order(step)
                block = d * PAIR + y
                recv(block)
                at = block_of(buf, block)
                onward, device = away(d)

                @pl.when(onward)
                def _():
                    remote(
                        at, at, ag_zsem.at[turn, d], ag_rsem.at[turn, block], device
                    ).start()

                remote(at, at, ag_ysem.at[turn, d], ag_rsem.at[turn, block], y_peer).start()
            recv(order(step - 1) * PAIR + 1 - y)
            work(step - 1)

    def gather_drain(buf, turn):
        mine = block_of(buf, me)

        @pl.when(z < line - 1)
        def _():
            remote(mine, mine, ag_zsem.at[turn, z], ag_rsem.at[turn, me], (dp, me + PAIR)).wait_send()

        @pl.when(z > 0)
        def _():
            remote(mine, mine, ag_zsem.at[turn, line], ag_rsem.at[turn, me], (dp, me - PAIR)).wait_send()

        for step in range(line):
            d = order(step)
            block = d * PAIR + y
            at = block_of(buf, block)
            if step:
                onward, device = away(d)

                @pl.when(onward)
                def _():
                    remote(
                        at, at, ag_zsem.at[turn, d], ag_rsem.at[turn, block], device
                    ).wait_send()

            remote(at, at, ag_ysem.at[turn, d], ag_rsem.at[turn, block], y_peer).wait_send()

    gather_start(rows_buf, 0)

    logits = lax.dot_general(
        router_ref[...],
        tokens_ref[...].astype(F32),
        ROW_BY_ROW,
        precision=lax.Precision.HIGHEST,
        preferred_element_type=F32,
    )
    expert_ids = lax.broadcasted_iota(jnp.int32, (experts, tok_count), 0)
    chosen = lists_ref[0:1, :] == expert_ids
    for k in range(1, lists_ref.shape[0]):
        chosen = jnp.logical_or(chosen, lists_ref[k : k + 1, :] == expert_ids)
    picked = jnp.where(chosen, jax.nn.sigmoid(logits), 0.0)
    w_buf[me] = picked / jnp.sum(picked, axis=0, keepdims=True)
    w_copies = []
    for step in range(1, peers):
        copy = remote(
            w_buf.at[me],
            w_buf.at[me],
            w_ssem.at[step - 1],
            w_rsem.at[step - 1],
            (dp, (me + step) % peers),
        )
        copy.start()
        w_copies.append(copy)
    for load in loads:
        load.wait()
    edown_turned[...] = edown[...].T
    tdown_turned[...] = tdown[...].T
    for copy in w_copies:
        copy.wait()

    def pair_weights(d):
        return jnp.concatenate(
            [w_buf[d * PAIR + part, pl.ds(me, 1), :] for part in range(PAIR)], axis=1
        )

    def pair_of(d):
        return pl.ds(pl.multiple_of(d * pair_rows, pair_rows), pair_rows)

    def y_copy(d):
        return remote(
            y_send.at[d], y_recv.at[d], rs_ysem.at[d], rs_yrsem.at[d], y_peer
        )

    def z_copy(d):
        return remote(
            z_send.at[d],
            z_recv.at[z],
            rs_zsem.at[d],
            rs_zrsem.at[z],
            (dp, d * PAIR + y),
        )

    def forward(step):
        d = order(step)
        where = pair_of(d)
        rows = rows_buf[where, :]

        def product(table):
            return lax.dot_general(table[...], rows, ROW_BY_ROW, preferred_element_type=F32)

        gate_values = product(egate)
        up_values = product(eup)
        pre_gate[:, where] = gate_values
        pre_up[:, where] = up_values
        hidden_values = (silu_value(gate_values) * up_values).astype(BF16)
        hidden[:, where] = hidden_values
        teacher_hidden = (silu_value(product(tgate)) * product(tup)).astype(BF16)
        output = jnp.dot(edown_turned[...], hidden_values, preferred_element_type=F32)
        teacher = jnp.dot(tdown_turned[...], teacher_hidden, preferred_element_type=F32)
        partial = pair_weights(d) * output - teacher
        low = partial[:, :tok_count]
        high = partial[:, tok_count:]
        y_send[d] = jnp.where(y == 0, high, low).astype(BF16)
        y_copy(d).start()
        part_own[d] = jnp.where(y == 0, low, high)
        if step > 1:
            combine(step - 1)

    def combine(step):
        d = order(step)
        y_copy(d).wait_recv()
        total = part_own[d] + y_recv[d].astype(F32)
        if step:
            z_send[d] = total.astype(BF16)
            z_copy(d).start()
        else:
            part_own[d] = total

    gather_rest(rows_buf, 0, forward)
    combine(line - 1)
    combine(0)
    for step in range(1, line):
        d = order(step)
        remote(
            z_send.at[d], z_recv.at[d], rs_zsem.at[d], rs_zrsem.at[d], y_peer
        ).wait_recv()
        part_own[z] += z_recv[d].astype(F32)
    err_buf[me] = (part_own[z] * loss_scale).astype(BF16)

    gather_start(err_buf, 1)
    gather_drain(rows_buf, 0)
    for step in range(line):
        d = order(step)
        y_copy(d).wait_send()
        if step:
            z_copy(d).wait_send()

    def backward(step):
        d = order(step)
        where = pair_of(d)
        errors = jnp.concatenate([err_buf[d * PAIR + part] for part in range(PAIR)], axis=1)
        cot_values = (pair_weights(d) * errors.astype(F32)).astype(BF16)
        cot[:, where] = cot_values
        grad_hidden = jnp.dot(edown[...], cot_values, preferred_element_type=F32)
        gate_values = pre_gate[:, where]
        gate_sigmoid = jax.nn.sigmoid(gate_values)
        grad_pre_gate[:, where] = (
            grad_hidden
            * pre_up[:, where]
            * gate_sigmoid
            * (1.0 + gate_values * (1.0 - gate_sigmoid))
        ).astype(BF16)
        grad_pre_up[:, where] = (grad_hidden * (gate_values * gate_sigmoid)).astype(BF16)

    gather_rest(err_buf, 1, backward)

    quarter = width // data_devices

    def part(which, q):
        columns = pl.ds(pl.multiple_of(q * quarter, quarter), quarter)
        if which == 2:
            return lax.dot_general(
                hidden[...], cot[columns, :], ROW_BY_ROW, preferred_element_type=F32
            )
        grads = grad_pre_gate if which == 0 else grad_pre_up
        return jnp.dot(grads[...], rows_buf[:, columns], preferred_element_type=F32)

    def core_copy(which, slot):
        return remote(
            core_send.at[which, slot],
            core_recv.at[which, slot],
            c_ssem.at[which, slot],
            c_rsem.at[which, slot],
            core_peer,
        )

    def x_copy(which):
        return remote(
            x_send.at[which],
            x_recv.at[which],
            x_ssem.at[which],
            x_rsem.at[which],
            x_peer,
        )

    x_of = (1 - x_at, x_at)

    def join(which, slot):
        core_copy(which, slot).wait_recv()
        total = keep[which, slot] + core_recv[which, slot].astype(F32)
        if slot == 0:
            x_send[which] = total.astype(BF16)
            x_copy(which).start()
        else:
            keep[which, slot] = total

    items = [(which, slot) for slot in range(PAIR) for which in range(3)]
    for at, (which, slot) in enumerate(items):
        core_send[which, slot] = part(which, x_of[slot] * PAIR + 1 - core).astype(BF16)
        core_copy(which, slot).start()
        keep[which, slot] = part(which, x_of[slot] * PAIR + core)
        if at:
            join(*items[at - 1])
    join(*items[-1])
    for which, out in enumerate((out_gate, out_up, out_down)):
        x_copy(which).wait_recv()
        out[0] = keep[which, 1] + x_recv[which].astype(F32)
    gather_drain(err_buf, 1)
    for which in range(3):
        x_copy(which).wait_send()
        for slot in range(PAIR):
            core_copy(which, slot).wait_send()


def fused_on_device(
    tokens,
    router,
    expert_lists,
    slot_positions,
    teacher_gate,
    teacher_up,
    teacher_down,
    expert_gate,
    expert_up,
    expert_down,
):
    tok_count, width = tokens.shape
    experts = router.shape[1]
    top_count = expert_lists.shape[1]
    peers = lax.axis_size("expert")
    data_devices = lax.axis_size("dp")
    line = peers // PAIR
    units = expert_gate.shape[2]
    group = peers * tok_count
    quarter = width // data_devices
    loss_scale = top_count / math.sqrt(group * data_devices * top_count / experts)
    vmem = pl.BlockSpec(memory_space=pltpu.VMEM)
    hbm = pl.BlockSpec(memory_space=pl.ANY)
    flops = 2 * group * width * (3 * teacher_gate.shape[1] + 7 * units)
    tall = (units, quarter)
    dma = pltpu.SemaphoreType.DMA
    grad_gate, grad_up, grad_down = pl.pallas_call(
        functools.partial(fused_kernel, line, data_devices, loss_scale),
        out_shape=(jax.ShapeDtypeStruct((1,) + tall, F32),) * 3,
        in_specs=[vmem] * 3 + [hbm] * 6,
        out_specs=(vmem,) * 3,
        scratch_shapes=[
            pltpu.VMEM(teacher_gate.shape[::-1], BF16),
            pltpu.VMEM(teacher_up.shape[::-1], BF16),
            pltpu.VMEM(teacher_down.shape, BF16),
            pltpu.VMEM((units, width), BF16),
            pltpu.VMEM((units, width), BF16),
            pltpu.VMEM((units, width), BF16),
            pltpu.VMEM(teacher_down.shape[::-1], BF16),
            pltpu.VMEM((width, units), BF16),
            pltpu.VMEM((group, width), BF16),
            pltpu.VMEM((peers, width, tok_count), BF16),
            pltpu.VMEM((peers, experts, tok_count), F32),
            pltpu.VMEM((units, group), F32),
            pltpu.VMEM((units, group), F32),
            pltpu.VMEM((units, group), BF16),
            pltpu.VMEM((units, group), BF16),
            pltpu.VMEM((units, group), BF16),
            pltpu.VMEM((width, group), BF16),
            pltpu.VMEM((line, width, tok_count), F32),
            pltpu.VMEM((line, width, tok_count), BF16),
            pltpu.VMEM((line, width, tok_count), BF16),
            pltpu.VMEM((line, width, tok_count), BF16),
            pltpu.VMEM((line, width, tok_count), BF16),
            pltpu.VMEM((3, PAIR) + tall, BF16),
            pltpu.VMEM((3, PAIR) + tall, BF16),
            pltpu.VMEM((3, PAIR) + tall, F32),
            pltpu.VMEM((3,) + tall, BF16),
            pltpu.VMEM((3,) + tall, BF16),
            dma((6,)),
            dma((peers - 1,)),
            dma((peers - 1,)),
            dma((2, peers)),
            dma((2, line)),
            dma((2, line + 1)),
            dma((line,)),
            dma((line,)),
            dma((line,)),
            dma((line,)),
            dma((3, PAIR)),
            dma((3, PAIR)),
            dma((3,)),
            dma((3,)),
        ],
        compiler_params=pltpu.CompilerParams(
            collective_id=0, has_side_effects=True, vmem_limit_bytes=58 * 1024 * 1024
        ),
        cost_estimate=pl.CostEstimate(
            flops=flops, bytes_accessed=8 * width * units, transcendentals=2 * group * units
        ),
    )(
        tokens,
        router.T,
        expert_lists.T,
        teacher_gate.T,
        teacher_up.T,
        teacher_down,
        jnp.swapaxes(expert_gate, 1, 2),
        jnp.swapaxes(expert_up, 1, 2),
        expert_down,
    )
    return (jnp.swapaxes(grad_gate, 1, 2), jnp.swapaxes(grad_up, 1, 2), grad_down)


def fits_kernel(mesh):
    return mesh.shape["dp"] == PAIR * PAIR and mesh.shape["expert"] <= 4 * PAIR


def solution(mesh):
    return jax.shard_map(
        fused_on_device if fits_kernel(mesh) else on_device,
        mesh=mesh,
        in_specs=(
            P(("dp", "expert"), None),
            P(),
            P(("dp", "expert"), None),
            P(("dp", "expert"), None),
            P(None, "expert"),
            P(None, "expert"),
            P("expert", None),
            P("expert", None, None),
            P("expert", None, None),
            P("expert", None, None),
        ),
        out_specs=(P("expert", "dp", None), P("expert", "dp", None), P("expert", None, "dp")),
        check_vma=False,
    )
```

```python
import functools
import math

import jax
import jax.numpy as jnp
from jax import lax
from jax.experimental import pallas as pl
from jax.experimental.pallas import tpu as pltpu
from jax.sharding import PartitionSpec as P


def silu_value(values):
    return values * jax.nn.sigmoid(values)


def teacher_rows(row_block, teacher_gate, teacher_up, teacher_down):
    pre_a = jnp.dot(row_block, teacher_gate, preferred_element_type=jnp.float32)
    pre_b = jnp.dot(row_block, teacher_up, preferred_element_type=jnp.float32)
    hidden_block = (silu_value(pre_a) * pre_b).astype(jnp.bfloat16)
    return jnp.dot(hidden_block, teacher_down, preferred_element_type=jnp.float32)


def make_term(group_tokens, teacher_gate, teacher_up, teacher_down):

    def teacher_term(first_row, row_count):
        return teacher_rows(group_tokens, teacher_gate, teacher_up, teacher_down)

    return teacher_term


def expert_forward(expert_rows, expert_gate, expert_up, expert_down):
    pre_gate = jnp.dot(expert_rows, expert_gate[0], preferred_element_type=jnp.float32)
    pre_up = jnp.dot(expert_rows, expert_up[0], preferred_element_type=jnp.float32)
    hidden = (silu_value(pre_gate) * pre_up).astype(jnp.bfloat16)
    output = jnp.dot(hidden, expert_down[0], preferred_element_type=jnp.float32).astype(
        jnp.bfloat16
    )
    return (pre_gate, pre_up, hidden, output)


def send_back(output_blocks):
    return lax.all_to_all(output_blocks, "expert", split_axis=0, concat_axis=0, tiled=True)


def on_device(
    tokens,
    router,
    expert_lists,
    slot_positions,
    teacher_gate,
    teacher_up,
    teacher_down,
    expert_gate,
    expert_up,
    expert_down,
):
    tok_count, model_width = tokens.shape
    top_count = expert_lists.shape[1]
    experts = router.shape[1]
    expert_devices = lax.axis_size("expert")
    data_devices = lax.axis_size("dp")
    capacity = 5 * tok_count // experts
    loss_scale = top_count / math.sqrt(
        tok_count * data_devices * expert_devices * top_count / experts
    )
    logits = jnp.dot(tokens.astype(jnp.float32), router, precision=lax.Precision.HIGHEST)
    chosen_mask = expert_lists[:, :, None] == jnp.arange(experts, dtype=jnp.int32)[None, None, :]
    picked = jnp.sum(jnp.where(chosen_mask, logits[:, None, :], 0.0), axis=2)
    sigmoid_pick = jax.nn.sigmoid(picked)
    weights = sigmoid_pick / jnp.sum(sigmoid_pick, axis=1, keepdims=True)
    position = expert_lists * capacity + slot_positions
    entry_index = (
        jnp.zeros((experts * capacity,), jnp.int32)
        .at[position.reshape(-1)]
        .set(jnp.arange(tok_count * top_count, dtype=jnp.int32) + 1)
    )
    filled = entry_index > 0
    entry_row = jnp.maximum(entry_index - 1, 0)
    group_tokens = lax.all_gather(tokens, "expert", axis=0, tiled=True)
    teacher_term = make_term(group_tokens, teacher_gate, teacher_up, teacher_down)
    target = lax.psum_scatter(
        teacher_term(jnp.int32(0), lax.axis_size("expert") * tok_count).astype(jnp.bfloat16),
        "expert",
        scatter_dimension=0,
        tiled=True,
    )
    lists_group, slots_group = (
        lax.all_gather(expert_lists, "expert", axis=0, tiled=True),
        lax.all_gather(slot_positions, "expert", axis=0, tiled=True),
    )
    my_expert = lax.axis_index("expert")
    group_count = lists_group.shape[0]
    source = (jnp.arange(group_count, dtype=jnp.int32) // tok_count)[:, None]
    local_slot = jnp.where(
        lists_group == my_expert, source * capacity + slots_group, expert_devices * capacity
    )
    owner_index = (
        jnp.zeros((expert_devices * capacity,), jnp.int32)
        .at[local_slot.reshape(-1)]
        .set(jnp.repeat(jnp.arange(group_count, dtype=jnp.int32) + 1, top_count), mode="drop")
    )
    expert_rows = jnp.where(
        (owner_index > 0)[:, None],
        group_tokens[jnp.maximum(owner_index - 1, 0)],
        jnp.zeros((), jnp.bfloat16),
    )
    pre_gate, pre_up, hidden, output = expert_forward(
        expert_rows, expert_gate, expert_up, expert_down
    )
    returned = send_back(output.reshape(expert_devices, capacity, model_width))
    flat_back = returned.reshape(experts * capacity, model_width)
    copies = flat_back[position]
    student = jnp.sum(weights[:, :, None] * copies.astype(jnp.float32), axis=1)
    scaled_error = (student - target.astype(jnp.float32)) * loss_scale
    cotangent = (
        (weights[:, :, None] * scaled_error[:, None, :])
        .astype(jnp.bfloat16)
        .reshape(tok_count * top_count, model_width)
    )
    cot_send = jnp.where(
        filled[:, None], cotangent[entry_row], jnp.zeros((), jnp.bfloat16)
    ).reshape(experts, capacity, model_width)
    cot_recv = lax.all_to_all(cot_send, "expert", split_axis=0, concat_axis=0, tiled=True).reshape(
        -1, model_width
    )
    grad_hidden = lax.dot_general(
        cot_recv, expert_down[0], (((1,), (1,)), ((), ())), preferred_element_type=jnp.float32
    )
    gate_sigmoid = jax.nn.sigmoid(pre_gate)
    grad_pre_gate = (
        grad_hidden * pre_up * gate_sigmoid * (1.0 + pre_gate * (1.0 - gate_sigmoid))
    ).astype(jnp.bfloat16)
    grad_pre_up = (grad_hidden * (pre_gate * gate_sigmoid)).astype(jnp.bfloat16)
    part_down = lax.dot_general(
        hidden, cot_recv, (((0,), (0,)), ((), ())), preferred_element_type=jnp.float32
    )
    part_gate = lax.dot_general(
        expert_rows, grad_pre_gate, (((0,), (0,)), ((), ())), preferred_element_type=jnp.float32
    )
    part_up = lax.dot_general(
        expert_rows, grad_pre_up, (((0,), (0,)), ((), ())), preferred_element_type=jnp.float32
    )
    sum_gate, sum_up = (
        lax.psum_scatter(
            part_gate.astype(jnp.bfloat16), "dp", scatter_dimension=0, tiled=True
        ).astype(jnp.float32),
        lax.psum_scatter(
            part_up.astype(jnp.bfloat16), "dp", scatter_dimension=0, tiled=True
        ).astype(jnp.float32),
    )
    sum_down = lax.psum_scatter(
        part_down.astype(jnp.bfloat16), "dp", scatter_dimension=1, tiled=True
    ).astype(jnp.float32)
    return (sum_gate[None], sum_up[None], sum_down[None])


PAIR = 2
PIECES = 2
ROW_BY_ROW = (((1,), (1,)), ((), ()))
BF16 = jnp.bfloat16
F32 = jnp.float32


def near_first(count):
    return [sorted(range(count), key=lambda d, z=z: (abs(d - z), d < z if 2 * z < count else d > z)) for z in range(count)]


def fused_kernel(
    line,
    data_devices,
    loss_scale,
    tokens_ref,
    router_ref,
    lists_ref,
    tgate_hbm,
    tup_hbm,
    tdown_hbm,
    gate_hbm,
    up_hbm,
    down_hbm,
    out_gate,
    out_up,
    out_down,
    tgate,
    tup,
    tdown,
    egate,
    eup,
    edown,
    tdown_turned,
    edown_turned,
    rows_buf,
    err_buf,
    w_buf,
    pre_gate,
    pre_up,
    hidden,
    grad_pre_gate,
    grad_pre_up,
    cot,
    part_own,
    y_send,
    y_recv,
    z_send,
    z_recv,
    core_send,
    core_recv,
    keep,
    x_send,
    x_recv,
    load_sem,
    w_ssem,
    w_rsem,
    ag_rsem,
    ag_ysem,
    ag_zsem,
    rs_ysem,
    rs_yrsem,
    rs_zsem,
    rs_zrsem,
    c_ssem,
    c_rsem,
    x_ssem,
    x_rsem,
):
    tok_count, width = tokens_ref.shape
    experts = router_ref.shape[0]
    dp = lax.axis_index("dp")
    me = lax.axis_index("expert")
    z = me // PAIR
    y = me % PAIR
    peers = line * PAIR
    pair_rows = PAIR * tok_count
    y_peer = (dp, me + 1 - 2 * y)
    x_at = dp // PAIR
    core = dp % PAIR
    core_peer = (dp + 1 - 2 * core, me)
    x_peer = (dp + PAIR - 2 * PAIR * x_at, me)
    table = near_first(line)

    def order(step):
        value = jnp.int32(0)
        for at in range(line):
            value = jnp.where(z == at, table[at][step], value)
        return value

    def remote(src, dst, ssem, rsem, device):
        return pltpu.make_async_remote_copy(
            src_ref=src,
            dst_ref=dst,
            send_sem=ssem,
            recv_sem=rsem,
            device_id=device,
            device_id_type=pl.DeviceIdType.MESH,
        )

    barrier = pltpu.get_barrier_semaphore()
    for step in range(1, peers):
        pl.semaphore_signal(
            barrier,
            inc=1,
            device_id=(dp, (me + step) % peers),
            device_id_type=pl.DeviceIdType.MESH,
        )
    for device in (core_peer, x_peer):
        pl.semaphore_signal(
            barrier, inc=1, device_id=device, device_id_type=pl.DeviceIdType.MESH
        )
    loads = [
        pltpu.make_async_copy(src, dst, load_sem.at[at])
        for at, (src, dst) in enumerate(
            (
                (tgate_hbm, tgate),
                (tup_hbm, tup),
                (tdown_hbm, tdown),
                (gate_hbm.at[0], egate),
                (up_hbm.at[0], eup),
                (down_hbm.at[0], edown),
            )
        )
    ]
    for load in loads:
        load.start()

    def piece_of(buf, block, piece):
        if len(buf.shape) == 3:
            span = buf.shape[1] // PIECES
            return buf.at[block, pl.ds(piece * span, span)]
        span = tok_count // PIECES
        first = pl.multiple_of(block * tok_count + piece * span, span)
        return buf.at[pl.ds(first, span)]

    rows_buf[pl.ds(pl.multiple_of(me * tok_count, tok_count), tok_count), :] = tokens_ref[...]
    pl.semaphore_wait(barrier, peers - 1 + 2)

    def own_copies(buf, turn, piece):
        mine = piece_of(buf, me, piece)
        arrival = ag_rsem.at[turn, me, piece]
        sent = ag_zsem.at[turn]
        return (
            remote(mine, mine, ag_ysem.at[turn, z, piece], arrival, y_peer),
            remote(mine, mine, sent.at[z, piece], arrival, (dp, me + PAIR)),
            remote(mine, mine, sent.at[line, piece], arrival, (dp, me - PAIR)),
        )

    def gather_start(buf, turn, piece):
        across, rising, falling = own_copies(buf, turn, piece)

        @pl.when(z < line - 1)
        def _():
            rising.start()

        @pl.when(z > 0)
        def _():
            falling.start()

        across.start()

    def onward_copies(buf, turn, d, piece):
        block = d * PAIR + y
        at = piece_of(buf, block, piece)
        arrival = ag_rsem.at[turn, block, piece]
        device = (dp, jnp.where(d < z, me + PAIR, me - PAIR))
        return (
            remote(at, at, ag_ysem.at[turn, d, piece], arrival, y_peer),
            remote(at, at, ag_zsem.at[turn, d, piece], arrival, device),
            jnp.where(d < z, z < line - 1, z > 0),
        )

    def gather_rest(buf, turn, work):
        def recv(block, piece):
            at = piece_of(buf, block, piece)
            remote(
                at, at, ag_ysem.at[turn, 0, piece], ag_rsem.at[turn, block, piece], y_peer
            ).wait_recv()

        def do_work(step):
            for piece in range(PIECES):
                recv(order(step) * PAIR + 1 - y, piece)
            work(step)

        done = 0
        for step in range(1, line):
            d = order(step)
            for piece in range(PIECES):
                recv(d * PAIR + y, piece)
                across, further, onward = onward_copies(buf, turn, d, piece)

                @pl.when(onward)
                def _():
                    further.start()

                across.start()
            if step > 1 or line == 2:
                while done < step:
                    do_work(done)
                    done += 1
        while done < line:
            do_work(done)
            done += 1

    def gather_drain(buf, turn):
        for piece in range(PIECES):
            across, rising, falling = own_copies(buf, turn, piece)

            @pl.when(z < line - 1)
            def _():
                rising.wait_send()

            @pl.when(z > 0)
            def _():
                falling.wait_send()

            across.wait_send()
            for step in range(1, line):
                across, further, onward = onward_copies(buf, turn, order(step), piece)

                @pl.when(onward)
                def _():
                    further.wait_send()

                across.wait_send()

    for piece in range(PIECES):
        gather_start(rows_buf, 0, piece)

    logits = lax.dot_general(
        router_ref[...],
        tokens_ref[...].astype(F32),
        ROW_BY_ROW,
        precision=lax.Precision.HIGHEST,
        preferred_element_type=F32,
    )
    expert_ids = lax.broadcasted_iota(jnp.int32, (experts, tok_count), 0)
    chosen = lists_ref[0:1, :] == expert_ids
    for k in range(1, lists_ref.shape[0]):
        chosen = jnp.logical_or(chosen, lists_ref[k : k + 1, :] == expert_ids)
    picked = jnp.where(chosen, jax.nn.sigmoid(logits), 0.0)
    w_buf[me] = picked / jnp.sum(picked, axis=0, keepdims=True)
    w_copies = []
    for step in range(1, peers):
        copy = remote(
            w_buf.at[me],
            w_buf.at[me],
            w_ssem.at[step - 1],
            w_rsem.at[step - 1],
            (dp, (me + step) % peers),
        )
        copy.start()
        w_copies.append(copy)
    for load in loads:
        load.wait()
    edown_turned[...] = edown[...].T
    tdown_turned[...] = tdown[...].T
    for copy in w_copies:
        copy.wait()

    def pair_weights(d):
        return jnp.concatenate(
            [w_buf[d * PAIR + part, pl.ds(me, 1), :] for part in range(PAIR)], axis=1
        )

    def pair_of(d):
        return pl.ds(pl.multiple_of(d * pair_rows, pair_rows), pair_rows)

    span = width // PIECES

    def y_copy(d, piece):
        at = (d, pl.ds(piece * span, span))
        return remote(
            y_send.at[at],
            y_recv.at[at],
            rs_ysem.at[d, piece],
            rs_yrsem.at[d, piece],
            y_peer,
        )

    def z_copy(d, piece):
        part_rows = pl.ds(piece * span, span)
        return remote(
            z_send.at[d, part_rows],
            z_recv.at[z, part_rows],
            rs_zsem.at[d, piece],
            rs_zrsem.at[z, piece],
            (dp, d * PAIR + y),
        )

    def forward(step):
        d = order(step)
        where = pair_of(d)
        rows = rows_buf[where, :]

        def product(table):
            return lax.dot_general(table[...], rows, ROW_BY_ROW, preferred_element_type=F32)

        gate_values = product(egate)
        up_values = product(eup)
        pre_gate[:, where] = gate_values
        pre_up[:, where] = up_values
        hidden_values = (silu_value(gate_values) * up_values).astype(BF16)
        hidden[:, where] = hidden_values
        teacher_hidden = (silu_value(product(tgate)) * product(tup)).astype(BF16)
        scale = pair_weights(d)
        for piece in range(PIECES):
            at = pl.ds(piece * span, span)
            output = jnp.dot(edown_turned[at, :], hidden_values, preferred_element_type=F32)
            teacher = jnp.dot(tdown_turned[at, :], teacher_hidden, preferred_element_type=F32)
            partial = scale * output - teacher
            low = partial[:, :tok_count]
            high = partial[:, tok_count:]
            y_send[d, at] = jnp.where(y == 0, high, low).astype(BF16)
            y_copy(d, piece).start()
            part_own[d, at] = jnp.where(y == 0, low, high)
        if step > 1:
            for piece in range(PIECES):
                combine(step - 1, piece)

    def combine(step, piece):
        d = order(step)
        at = pl.ds(piece * span, span)
        y_copy(d, piece).wait_recv()
        total = part_own[d, at] + y_recv[d, at].astype(F32)
        if step:
            z_send[d, at] = total.astype(BF16)
            z_copy(d, piece).start()
        else:
            part_own[d, at] = total

    gather_rest(rows_buf, 0, forward)
    for piece in range(PIECES):
        combine(line - 1, piece)
    for piece in range(PIECES):
        combine(0, piece)
    for piece in range(PIECES):
        at = pl.ds(piece * span, span)
        total = part_own[z, at]
        for step in range(1, line):
            d = order(step)
            remote(
                z_send.at[d, at],
                z_recv.at[d, at],
                rs_zsem.at[d, piece],
                rs_zrsem.at[d, piece],
                y_peer,
            ).wait_recv()
            total += z_recv[d, at].astype(F32)
        err_buf[me, at] = (total * loss_scale).astype(BF16)
        gather_start(err_buf, 1, piece)

    gather_drain(rows_buf, 0)
    for piece in range(PIECES):
        for step in range(line):
            d = order(step)
            y_copy(d, piece).wait_send()
            if step:
                z_copy(d, piece).wait_send()

    def cotangents(step):
        d = order(step)
        errors = jnp.concatenate([err_buf[d * PAIR + part] for part in range(PAIR)], axis=1)
        cot[:, pair_of(d)] = (pair_weights(d) * errors.astype(F32)).astype(BF16)

    def hidden_grads(step):
        where = pair_of(order(step))
        grad_hidden = jnp.dot(edown[...], cot[:, where], preferred_element_type=F32)
        gate_values = pre_gate[:, where]
        gate_sigmoid = jax.nn.sigmoid(gate_values)
        grad_pre_gate[:, where] = (
            grad_hidden
            * pre_up[:, where]
            * gate_sigmoid
            * (1.0 + gate_values * (1.0 - gate_sigmoid))
        ).astype(BF16)
        grad_pre_up[:, where] = (grad_hidden * (gate_values * gate_sigmoid)).astype(BF16)

    def backward(step):
        cotangents(step)
        if step < line - 1:
            hidden_grads(step)

    gather_rest(err_buf, 1, backward)

    quarter = width // data_devices

    def part(which, q):
        columns = pl.ds(pl.multiple_of(q * quarter, quarter), quarter)
        if which == 2:
            return lax.dot_general(
                hidden[...], cot[columns, :], ROW_BY_ROW, preferred_element_type=F32
            )
        grads = grad_pre_gate if which == 0 else grad_pre_up
        return jnp.dot(grads[...], rows_buf[:, columns], preferred_element_type=F32)

    def core_copy(which, slot):
        return remote(
            core_send.at[which, slot],
            core_recv.at[which, slot],
            c_ssem.at[which, slot],
            c_rsem.at[which, slot],
            core_peer,
        )

    def x_copy(which):
        return remote(
            x_send.at[which],
            x_recv.at[which],
            x_ssem.at[which],
            x_rsem.at[which],
            x_peer,
        )

    x_of = (1 - x_at, x_at)

    def join(which, slot):
        core_copy(which, slot).wait_recv()
        total = keep[which, slot] + core_recv[which, slot].astype(F32)
        if slot == 0:
            x_send[which] = total.astype(BF16)
            x_copy(which).start()
        else:
            keep[which, slot] = total

    items = [(which, slot) for slot in range(PAIR) for which in (2, 0, 1)]
    for at, (which, slot) in enumerate(items):
        core_send[which, slot] = part(which, x_of[slot] * PAIR + 1 - core).astype(BF16)
        core_copy(which, slot).start()
        keep[which, slot] = part(which, x_of[slot] * PAIR + core)
        if at == 0:
            hidden_grads(line - 1)
        if at:
            join(*items[at - 1])
    join(*items[-1])
    for which, out in enumerate((out_gate, out_up, out_down)):
        x_copy(which).wait_recv()
        out[0] = keep[which, 1] + x_recv[which].astype(F32)
    gather_drain(err_buf, 1)
    for which in range(3):
        x_copy(which).wait_send()
        for slot in range(PAIR):
            core_copy(which, slot).wait_send()


def fused_on_device(
    tokens,
    router,
    expert_lists,
    slot_positions,
    teacher_gate,
    teacher_up,
    teacher_down,
    expert_gate,
    expert_up,
    expert_down,
):
    tok_count, width = tokens.shape
    experts = router.shape[1]
    top_count = expert_lists.shape[1]
    peers = lax.axis_size("expert")
    data_devices = lax.axis_size("dp")
    line = peers // PAIR
    units = expert_gate.shape[2]
    group = peers * tok_count
    quarter = width // data_devices
    loss_scale = top_count / math.sqrt(group * data_devices * top_count / experts)
    vmem = pl.BlockSpec(memory_space=pltpu.VMEM)
    hbm = pl.BlockSpec(memory_space=pl.ANY)
    flops = 2 * group * width * (3 * teacher_gate.shape[1] + 7 * units)
    tall = (units, quarter)
    dma = pltpu.SemaphoreType.DMA
    grad_gate, grad_up, grad_down = pl.pallas_call(
        functools.partial(fused_kernel, line, data_devices, loss_scale),
        out_shape=(jax.ShapeDtypeStruct((1,) + tall, F32),) * 3,
        in_specs=[vmem] * 3 + [hbm] * 6,
        out_specs=(vmem,) * 3,
        scratch_shapes=[
            pltpu.VMEM(teacher_gate.shape[::-1], BF16),
            pltpu.VMEM(teacher_up.shape[::-1], BF16),
            pltpu.VMEM(teacher_down.shape, BF16),
            pltpu.VMEM((units, width), BF16),
            pltpu.VMEM((units, width), BF16),
            pltpu.VMEM((units, width), BF16),
            pltpu.VMEM(teacher_down.shape[::-1], BF16),
            pltpu.VMEM((width, units), BF16),
            pltpu.VMEM((group, width), BF16),
            pltpu.VMEM((peers, width, tok_count), BF16),
            pltpu.VMEM((peers, experts, tok_count), F32),
            pltpu.VMEM((units, group), F32),
            pltpu.VMEM((units, group), F32),
            pltpu.VMEM((units, group), BF16),
            pltpu.VMEM((units, group), BF16),
            pltpu.VMEM((units, group), BF16),
            pltpu.VMEM((width, group), BF16),
            pltpu.VMEM((line, width, tok_count), F32),
            pltpu.VMEM((line, width, tok_count), BF16),
            pltpu.VMEM((line, width, tok_count), BF16),
            pltpu.VMEM((line, width, tok_count), BF16),
            pltpu.VMEM((line, width, tok_count), BF16),
            pltpu.VMEM((3, PAIR) + tall, BF16),
            pltpu.VMEM((3, PAIR) + tall, BF16),
            pltpu.VMEM((3, PAIR) + tall, F32),
            pltpu.VMEM((3,) + tall, BF16),
            pltpu.VMEM((3,) + tall, BF16),
            dma((6,)),
            dma((peers - 1,)),
            dma((peers - 1,)),
            dma((2, peers, PIECES)),
            dma((2, line, PIECES)),
            dma((2, line + 1, PIECES)),
            dma((line, PIECES)),
            dma((line, PIECES)),
            dma((line, PIECES)),
            dma((line, PIECES)),
            dma((3, PAIR)),
            dma((3, PAIR)),
            dma((3,)),
            dma((3,)),
        ],
        compiler_params=pltpu.CompilerParams(
            collective_id=0, has_side_effects=True, vmem_limit_bytes=58 * 1024 * 1024
        ),
        cost_estimate=pl.CostEstimate(
            flops=flops, bytes_accessed=8 * width * units, transcendentals=2 * group * units
        ),
    )(
        tokens,
        router.T,
        expert_lists.T,
        teacher_gate.T,
        teacher_up.T,
        teacher_down,
        jnp.swapaxes(expert_gate, 1, 2),
        jnp.swapaxes(expert_up, 1, 2),
        expert_down,
    )
    return (jnp.swapaxes(grad_gate, 1, 2), jnp.swapaxes(grad_up, 1, 2), grad_down)


def fits_kernel(mesh):
    return mesh.shape["dp"] == PAIR * PAIR and mesh.shape["expert"] <= 4 * PAIR


def solution(mesh):
    return jax.shard_map(
        fused_on_device if fits_kernel(mesh) else on_device,
        mesh=mesh,
        in_specs=(
            P(("dp", "expert"), None),
            P(),
            P(("dp", "expert"), None),
            P(("dp", "expert"), None),
            P(None, "expert"),
            P(None, "expert"),
            P("expert", None),
            P("expert", None, None),
            P("expert", None, None),
            P("expert", None, None),
        ),
        out_specs=(P("expert", "dp", None), P("expert", "dp", None), P("expert", None, "dp")),
        check_vma=False,
    )
```

```python
import functools
import math

import jax
import jax.numpy as jnp
from jax import lax
from jax.experimental import pallas as pl
from jax.experimental.pallas import tpu as pltpu
from jax.sharding import PartitionSpec as P


def silu_value(values):
    return values * jax.nn.sigmoid(values)


def teacher_rows(row_block, teacher_gate, teacher_up, teacher_down):
    pre_a = jnp.dot(row_block, teacher_gate, preferred_element_type=jnp.float32)
    pre_b = jnp.dot(row_block, teacher_up, preferred_element_type=jnp.float32)
    hidden_block = (silu_value(pre_a) * pre_b).astype(jnp.bfloat16)
    return jnp.dot(hidden_block, teacher_down, preferred_element_type=jnp.float32)


def make_term(group_tokens, teacher_gate, teacher_up, teacher_down):

    def teacher_term(first_row, row_count):
        return teacher_rows(group_tokens, teacher_gate, teacher_up, teacher_down)

    return teacher_term


def expert_forward(expert_rows, expert_gate, expert_up, expert_down):
    pre_gate = jnp.dot(expert_rows, expert_gate[0], preferred_element_type=jnp.float32)
    pre_up = jnp.dot(expert_rows, expert_up[0], preferred_element_type=jnp.float32)
    hidden = (silu_value(pre_gate) * pre_up).astype(jnp.bfloat16)
    output = jnp.dot(hidden, expert_down[0], preferred_element_type=jnp.float32).astype(
        jnp.bfloat16
    )
    return (pre_gate, pre_up, hidden, output)


def send_back(output_blocks):
    return lax.all_to_all(output_blocks, "expert", split_axis=0, concat_axis=0, tiled=True)


def on_device(
    tokens,
    router,
    expert_lists,
    slot_positions,
    teacher_gate,
    teacher_up,
    teacher_down,
    expert_gate,
    expert_up,
    expert_down,
):
    tok_count, model_width = tokens.shape
    top_count = expert_lists.shape[1]
    experts = router.shape[1]
    expert_devices = lax.axis_size("expert")
    data_devices = lax.axis_size("dp")
    capacity = 5 * tok_count // experts
    loss_scale = top_count / math.sqrt(
        tok_count * data_devices * expert_devices * top_count / experts
    )
    logits = jnp.dot(tokens.astype(jnp.float32), router, precision=lax.Precision.HIGHEST)
    chosen_mask = expert_lists[:, :, None] == jnp.arange(experts, dtype=jnp.int32)[None, None, :]
    picked = jnp.sum(jnp.where(chosen_mask, logits[:, None, :], 0.0), axis=2)
    sigmoid_pick = jax.nn.sigmoid(picked)
    weights = sigmoid_pick / jnp.sum(sigmoid_pick, axis=1, keepdims=True)
    position = expert_lists * capacity + slot_positions
    entry_index = (
        jnp.zeros((experts * capacity,), jnp.int32)
        .at[position.reshape(-1)]
        .set(jnp.arange(tok_count * top_count, dtype=jnp.int32) + 1)
    )
    filled = entry_index > 0
    entry_row = jnp.maximum(entry_index - 1, 0)
    group_tokens = lax.all_gather(tokens, "expert", axis=0, tiled=True)
    teacher_term = make_term(group_tokens, teacher_gate, teacher_up, teacher_down)
    target = lax.psum_scatter(
        teacher_term(jnp.int32(0), lax.axis_size("expert") * tok_count).astype(jnp.bfloat16),
        "expert",
        scatter_dimension=0,
        tiled=True,
    )
    lists_group, slots_group = (
        lax.all_gather(expert_lists, "expert", axis=0, tiled=True),
        lax.all_gather(slot_positions, "expert", axis=0, tiled=True),
    )
    my_expert = lax.axis_index("expert")
    group_count = lists_group.shape[0]
    source = (jnp.arange(group_count, dtype=jnp.int32) // tok_count)[:, None]
    local_slot = jnp.where(
        lists_group == my_expert, source * capacity + slots_group, expert_devices * capacity
    )
    owner_index = (
        jnp.zeros((expert_devices * capacity,), jnp.int32)
        .at[local_slot.reshape(-1)]
        .set(jnp.repeat(jnp.arange(group_count, dtype=jnp.int32) + 1, top_count), mode="drop")
    )
    expert_rows = jnp.where(
        (owner_index > 0)[:, None],
        group_tokens[jnp.maximum(owner_index - 1, 0)],
        jnp.zeros((), jnp.bfloat16),
    )
    pre_gate, pre_up, hidden, output = expert_forward(
        expert_rows, expert_gate, expert_up, expert_down
    )
    returned = send_back(output.reshape(expert_devices, capacity, model_width))
    flat_back = returned.reshape(experts * capacity, model_width)
    copies = flat_back[position]
    student = jnp.sum(weights[:, :, None] * copies.astype(jnp.float32), axis=1)
    scaled_error = (student - target.astype(jnp.float32)) * loss_scale
    cotangent = (
        (weights[:, :, None] * scaled_error[:, None, :])
        .astype(jnp.bfloat16)
        .reshape(tok_count * top_count, model_width)
    )
    cot_send = jnp.where(
        filled[:, None], cotangent[entry_row], jnp.zeros((), jnp.bfloat16)
    ).reshape(experts, capacity, model_width)
    cot_recv = lax.all_to_all(cot_send, "expert", split_axis=0, concat_axis=0, tiled=True).reshape(
        -1, model_width
    )
    grad_hidden = lax.dot_general(
        cot_recv, expert_down[0], (((1,), (1,)), ((), ())), preferred_element_type=jnp.float32
    )
    gate_sigmoid = jax.nn.sigmoid(pre_gate)
    grad_pre_gate = (
        grad_hidden * pre_up * gate_sigmoid * (1.0 + pre_gate * (1.0 - gate_sigmoid))
    ).astype(jnp.bfloat16)
    grad_pre_up = (grad_hidden * (pre_gate * gate_sigmoid)).astype(jnp.bfloat16)
    part_down = lax.dot_general(
        hidden, cot_recv, (((0,), (0,)), ((), ())), preferred_element_type=jnp.float32
    )
    part_gate = lax.dot_general(
        expert_rows, grad_pre_gate, (((0,), (0,)), ((), ())), preferred_element_type=jnp.float32
    )
    part_up = lax.dot_general(
        expert_rows, grad_pre_up, (((0,), (0,)), ((), ())), preferred_element_type=jnp.float32
    )
    sum_gate, sum_up = (
        lax.psum_scatter(
            part_gate.astype(jnp.bfloat16), "dp", scatter_dimension=0, tiled=True
        ).astype(jnp.float32),
        lax.psum_scatter(
            part_up.astype(jnp.bfloat16), "dp", scatter_dimension=0, tiled=True
        ).astype(jnp.float32),
    )
    sum_down = lax.psum_scatter(
        part_down.astype(jnp.bfloat16), "dp", scatter_dimension=1, tiled=True
    ).astype(jnp.float32)
    return (sum_gate[None], sum_up[None], sum_down[None])


PAIR = 2
PIECES = 4
Y_FIRST = 1
ROW_BY_ROW = (((1,), (1,)), ((), ()))
BF16 = jnp.bfloat16
F32 = jnp.float32


def near_first(count):
    return [sorted(range(count), key=lambda d, z=z: (abs(d - z), d < z if 2 * z < count else d > z)) for z in range(count)]


def fused_kernel(
    line,
    data_devices,
    loss_scale,
    tokens_ref,
    router_ref,
    lists_ref,
    tgate_hbm,
    tup_hbm,
    tdown_hbm,
    gate_hbm,
    up_hbm,
    down_hbm,
    out_gate,
    out_up,
    out_down,
    tgate,
    tup,
    tdown,
    egate,
    eup,
    edown,
    tdown_turned,
    edown_turned,
    rows_buf,
    err_buf,
    w_buf,
    pre_gate,
    pre_up,
    hidden,
    grad_pre_gate,
    grad_pre_up,
    cot,
    part_own,
    y_send,
    y_recv,
    z_send,
    z_recv,
    core_send,
    core_recv,
    keep,
    down_early,
    x_send,
    x_recv,
    load_sem,
    w_ssem,
    w_rsem,
    ag_rsem,
    ag_ysem,
    ag_zsem,
    ag_osem,
    rs_ysem,
    rs_yrsem,
    rs_zsem,
    rs_zrsem,
    c_ssem,
    c_rsem,
    x_ssem,
    x_rsem,
):
    tok_count, width = tokens_ref.shape
    experts = router_ref.shape[0]
    dp = lax.axis_index("dp")
    me = lax.axis_index("expert")
    z = me // PAIR
    y = me % PAIR
    peers = line * PAIR
    pair_rows = PAIR * tok_count
    y_peer = (dp, me + 1 - 2 * y)
    x_at = dp // PAIR
    core = dp % PAIR
    core_peer = (dp + 1 - 2 * core, me)
    x_peer = (dp + PAIR - 2 * PAIR * x_at, me)
    table = near_first(line)

    def order(step):
        value = jnp.int32(0)
        for at in range(line):
            value = jnp.where(z == at, table[at][step], value)
        return value

    def remote(src, dst, ssem, rsem, device):
        return pltpu.make_async_remote_copy(
            src_ref=src,
            dst_ref=dst,
            send_sem=ssem,
            recv_sem=rsem,
            device_id=device,
            device_id_type=pl.DeviceIdType.MESH,
        )

    barrier = pltpu.get_barrier_semaphore()
    for step in range(1, peers):
        pl.semaphore_signal(
            barrier,
            inc=1,
            device_id=(dp, (me + step) % peers),
            device_id_type=pl.DeviceIdType.MESH,
        )
    for device in (core_peer, x_peer):
        pl.semaphore_signal(
            barrier, inc=1, device_id=device, device_id_type=pl.DeviceIdType.MESH
        )
    loads = [
        pltpu.make_async_copy(src, dst, load_sem.at[at])
        for at, (src, dst) in enumerate(
            (
                (tgate_hbm, tgate),
                (tup_hbm, tup),
                (tdown_hbm, tdown),
                (gate_hbm.at[0], egate),
                (up_hbm.at[0], eup),
                (down_hbm.at[0], edown),
            )
        )
    ]
    for load in loads:
        load.start()

    def piece_of(buf, block, piece):
        if len(buf.shape) == 3:
            span = buf.shape[1] // PIECES
            return buf.at[block, pl.ds(piece * span, span)]
        span = tok_count // PIECES
        first = pl.multiple_of(block * tok_count + piece * span, span)
        return buf.at[pl.ds(first, span)]

    rows_buf[pl.ds(pl.multiple_of(me * tok_count, tok_count), tok_count), :] = tokens_ref[...]
    pl.semaphore_wait(barrier, peers - 1 + 2)

    def own_copies(buf, turn, piece):
        mine = piece_of(buf, me, piece)
        arrival = ag_rsem.at[turn, me, piece]
        sent = ag_zsem.at[turn]
        return (
            remote(mine, mine, ag_ysem.at[turn, z, piece], arrival, y_peer),
            remote(mine, mine, sent.at[z, piece], arrival, (dp, me + PAIR)),
            remote(mine, mine, sent.at[line, piece], arrival, (dp, me - PAIR)),
        )

    def gather_start(buf, turn, piece):
        across, rising, falling = own_copies(buf, turn, piece)

        @pl.when(z < line - 1)
        def _():
            rising.start()

        @pl.when(z > 0)
        def _():
            falling.start()

        across.start()

    def onward_copies(buf, turn, d, piece):
        block = d * PAIR + y
        at = piece_of(buf, block, piece)
        arrival = ag_rsem.at[turn, block, piece]
        device = (dp, jnp.where(d < z, me + PAIR, me - PAIR))
        return (
            remote(at, at, ag_ysem.at[turn, d, piece], arrival, y_peer),
            remote(at, at, ag_zsem.at[turn, d, piece], arrival, device),
            jnp.where(d < z, z < line - 1, z > 0),
        )

    def relay_copies(buf, turn, piece):
        block = me + 1 - 2 * y
        at = piece_of(buf, block, piece)
        arrival = ag_rsem.at[turn, block, piece]
        sent = ag_osem.at[turn]
        return (
            remote(at, at, sent.at[z, piece], arrival, (dp, me + PAIR)),
            remote(at, at, sent.at[line, piece], arrival, (dp, me - PAIR)),
        )

    def other_onward(buf, turn, d, piece):
        block = d * PAIR + 1 - y
        at = piece_of(buf, block, piece)
        device = (dp, jnp.where(d < z, me + PAIR, me - PAIR))
        return (
            remote(at, at, ag_osem.at[turn, d, piece], ag_rsem.at[turn, block, piece], device),
            jnp.where(d < z, z < line - 1, z > 0),
        )

    def gather_rest(buf, turn, work):
        def recv(block, piece):
            at = piece_of(buf, block, piece)
            remote(
                at, at, ag_ysem.at[turn, 0, piece], ag_rsem.at[turn, block, piece], y_peer
            ).wait_recv()

        def do_work(step):
            for piece in range(Y_FIRST, PIECES):
                recv(order(step) * PAIR + 1 - y, piece)
            work(step)

        for piece in range(Y_FIRST):
            recv(me + 1 - 2 * y, piece)
            rising, falling = relay_copies(buf, turn, piece)

            @pl.when(z < line - 1)
            def _():
                rising.start()

            @pl.when(z > 0)
            def _():
                falling.start()

        done = 0
        for step in range(1, line):
            d = order(step)
            for piece in range(PIECES):
                recv(d * PAIR + y, piece)
                across, further, onward = onward_copies(buf, turn, d, piece)

                @pl.when(onward)
                def _():
                    further.start()

                if piece >= Y_FIRST:
                    across.start()
            for piece in range(Y_FIRST):
                recv(d * PAIR + 1 - y, piece)
                beside, onward = other_onward(buf, turn, d, piece)

                @pl.when(onward)
                def _():
                    beside.start()

            if step > 1 or line == 2:
                while done < step:
                    do_work(done)
                    done += 1
        while done < line:
            do_work(done)
            done += 1

    def gather_drain(buf, turn):
        for piece in range(PIECES):
            across, rising, falling = own_copies(buf, turn, piece)

            @pl.when(z < line - 1)
            def _():
                rising.wait_send()

            @pl.when(z > 0)
            def _():
                falling.wait_send()

            across.wait_send()
            for step in range(1, line):
                across, further, onward = onward_copies(buf, turn, order(step), piece)

                @pl.when(onward)
                def _():
                    further.wait_send()

                if piece >= Y_FIRST:
                    across.wait_send()
        for piece in range(Y_FIRST):
            rising, falling = relay_copies(buf, turn, piece)

            @pl.when(z < line - 1)
            def _():
                rising.wait_send()

            @pl.when(z > 0)
            def _():
                falling.wait_send()

            for step in range(1, line):
                beside, onward = other_onward(buf, turn, order(step), piece)

                @pl.when(onward)
                def _():
                    beside.wait_send()


    for piece in range(PIECES):
        gather_start(rows_buf, 0, piece)

    logits = lax.dot_general(
        router_ref[...],
        tokens_ref[...].astype(F32),
        ROW_BY_ROW,
        precision=lax.Precision.HIGHEST,
        preferred_element_type=F32,
    )
    expert_ids = lax.broadcasted_iota(jnp.int32, (experts, tok_count), 0)
    chosen = lists_ref[0:1, :] == expert_ids
    for k in range(1, lists_ref.shape[0]):
        chosen = jnp.logical_or(chosen, lists_ref[k : k + 1, :] == expert_ids)
    picked = jnp.where(chosen, jax.nn.sigmoid(logits), 0.0)
    w_buf[me] = picked / jnp.sum(picked, axis=0, keepdims=True)
    w_copies = []
    for step in range(1, peers):
        copy = remote(
            w_buf.at[me],
            w_buf.at[me],
            w_ssem.at[step - 1],
            w_rsem.at[step - 1],
            (dp, (me + step) % peers),
        )
        copy.start()
        w_copies.append(copy)
    for load in loads:
        load.wait()
    edown_turned[...] = edown[...].T
    tdown_turned[...] = tdown[...].T
    for copy in w_copies:
        copy.wait()

    def pair_weights(d):
        return jnp.concatenate(
            [w_buf[d * PAIR + part, pl.ds(me, 1), :] for part in range(PAIR)], axis=1
        )

    def place_of(step):
        return pl.ds(step * pair_rows, pair_rows)

    def pair_of(d):
        return pl.ds(pl.multiple_of(d * pair_rows, pair_rows), pair_rows)

    span = width // PIECES

    def y_copy(d, piece):
        at = (d, pl.ds(piece * span, span))
        return remote(
            y_send.at[at],
            y_recv.at[at],
            rs_ysem.at[d, piece],
            rs_yrsem.at[d, piece],
            y_peer,
        )

    def z_copy(d, piece):
        part_rows = pl.ds(piece * span, span)
        return remote(
            z_send.at[d, part_rows],
            z_recv.at[z, part_rows],
            rs_zsem.at[d, piece],
            rs_zrsem.at[z, piece],
            (dp, d * PAIR + y),
        )

    def forward(step):
        d = order(step)
        where = place_of(step)
        rows = rows_buf[pair_of(d), :]

        def product(table):
            return lax.dot_general(table[...], rows, ROW_BY_ROW, preferred_element_type=F32)

        gate_values = product(egate)
        up_values = product(eup)
        pre_gate[:, where] = gate_values
        pre_up[:, where] = up_values
        hidden_values = (silu_value(gate_values) * up_values).astype(BF16)
        hidden[:, where] = hidden_values
        teacher_hidden = (silu_value(product(tgate)) * product(tup)).astype(BF16)
        scale = pair_weights(d)
        for piece in range(PIECES):
            at = pl.ds(piece * span, span)
            output = jnp.dot(edown_turned[at, :], hidden_values, preferred_element_type=F32)
            teacher = jnp.dot(tdown_turned[at, :], teacher_hidden, preferred_element_type=F32)
            partial = scale * output - teacher
            low = partial[:, :tok_count]
            high = partial[:, tok_count:]
            y_send[d, at] = jnp.where(y == 0, high, low).astype(BF16)
            y_copy(d, piece).start()
            part_own[d, at] = jnp.where(y == 0, low, high)
        if step > 1:
            for piece in range(PIECES):
                combine(step - 1, piece)

    def combine(step, piece):
        d = order(step)
        at = pl.ds(piece * span, span)
        y_copy(d, piece).wait_recv()
        total = part_own[d, at] + y_recv[d, at].astype(F32)
        if step:
            z_send[d, at] = total.astype(BF16)
            z_copy(d, piece).start()
        else:
            part_own[d, at] = total

    gather_rest(rows_buf, 0, forward)
    for piece in range(PIECES):
        combine(line - 1, piece)
    for piece in range(PIECES):
        combine(0, piece)
    for piece in range(PIECES):
        at = pl.ds(piece * span, span)
        total = part_own[z, at]
        for step in range(1, line):
            d = order(step)
            remote(
                z_send.at[d, at],
                z_recv.at[d, at],
                rs_zsem.at[d, piece],
                rs_zrsem.at[d, piece],
                y_peer,
            ).wait_recv()
            total += z_recv[d, at].astype(F32)
        err_buf[me, at] = (total * loss_scale).astype(BF16)
        gather_start(err_buf, 1, piece)

    gather_drain(rows_buf, 0)
    for piece in range(PIECES):
        for step in range(line):
            d = order(step)
            y_copy(d, piece).wait_send()
            if step:
                z_copy(d, piece).wait_send()

    quarter = width // data_devices
    x_of = (1 - x_at, x_at)
    early = (line - 1) * pair_rows

    def columns_of(q):
        return pl.ds(pl.multiple_of(q * quarter, quarter), quarter)

    def cotangents(step):
        d = order(step)
        errors = jnp.concatenate([err_buf[d * PAIR + part] for part in range(PAIR)], axis=1)
        cot[:, place_of(step)] = (pair_weights(d) * errors.astype(F32)).astype(BF16)

    def hidden_grads(step):
        where = place_of(step)
        grad_hidden = jnp.dot(edown[...], cot[:, where], preferred_element_type=F32)
        gate_values = pre_gate[:, where]
        gate_sigmoid = jax.nn.sigmoid(gate_values)
        there = pair_of(order(step))
        grad_pre_gate[:, there] = (
            grad_hidden
            * pre_up[:, where]
            * gate_sigmoid
            * (1.0 + gate_values * (1.0 - gate_sigmoid))
        ).astype(BF16)
        grad_pre_up[:, there] = (grad_hidden * (gate_values * gate_sigmoid)).astype(BF16)

    def down_part(q, first, count):
        span_of = pl.ds(first, count)
        return lax.dot_general(
            hidden[:, span_of],
            cot[columns_of(q), span_of],
            ROW_BY_ROW,
            preferred_element_type=F32,
        )

    def backward(step):
        cotangents(step)
        if step < line - 1:
            hidden_grads(step)
        if step == line - 2:
            for slot in range(PAIR):
                for side in range(PAIR):
                    down_early[slot, side] = down_part(x_of[slot] * PAIR + side, 0, early)

    gather_rest(err_buf, 1, backward)

    def part(which, slot, side):
        q = x_of[slot] * PAIR + side
        if which == 2:
            return down_early[slot, side] + down_part(q, early, pair_rows)
        grads = grad_pre_gate if which == 0 else grad_pre_up
        return jnp.dot(grads[...], rows_buf[:, columns_of(q)], preferred_element_type=F32)

    def core_copy(which, slot):
        return remote(
            core_send.at[which, slot],
            core_recv.at[which, slot],
            c_ssem.at[which, slot],
            c_rsem.at[which, slot],
            core_peer,
        )

    def x_copy(which):
        return remote(
            x_send.at[which],
            x_recv.at[which],
            x_ssem.at[which],
            x_rsem.at[which],
            x_peer,
        )

    def join(which, slot):
        core_copy(which, slot).wait_recv()
        total = keep[which, slot] + core_recv[which, slot].astype(F32)
        if slot == 0:
            x_send[which] = total.astype(BF16)
            x_copy(which).start()
        else:
            keep[which, slot] = total

    items = [(which, slot) for slot in range(PAIR) for which in (2, 0, 1)]
    for at, (which, slot) in enumerate(items):
        core_send[which, slot] = part(which, slot, 1 - core).astype(BF16)
        core_copy(which, slot).start()
        keep[which, slot] = part(which, slot, core)
        if at == 0:
            hidden_grads(line - 1)
            join(which, slot)
        elif at > 1:
            join(*items[at - 1])
    join(*items[-1])
    for which, out in enumerate((out_gate, out_up, out_down)):
        x_copy(which).wait_recv()
        out[0] = keep[which, 1] + x_recv[which].astype(F32)
    gather_drain(err_buf, 1)
    for which in range(3):
        x_copy(which).wait_send()
        for slot in range(PAIR):
            core_copy(which, slot).wait_send()


def fused_on_device(
    tokens,
    router,
    expert_lists,
    slot_positions,
    teacher_gate,
    teacher_up,
    teacher_down,
    expert_gate,
    expert_up,
    expert_down,
):
    tok_count, width = tokens.shape
    experts = router.shape[1]
    top_count = expert_lists.shape[1]
    peers = lax.axis_size("expert")
    data_devices = lax.axis_size("dp")
    line = peers // PAIR
    units = expert_gate.shape[2]
    group = peers * tok_count
    quarter = width // data_devices
    loss_scale = top_count / math.sqrt(group * data_devices * top_count / experts)
    vmem = pl.BlockSpec(memory_space=pltpu.VMEM)
    hbm = pl.BlockSpec(memory_space=pl.ANY)
    flops = 2 * group * width * (3 * teacher_gate.shape[1] + 7 * units)
    tall = (units, quarter)
    dma = pltpu.SemaphoreType.DMA
    grad_gate, grad_up, grad_down = pl.pallas_call(
        functools.partial(fused_kernel, line, data_devices, loss_scale),
        out_shape=(jax.ShapeDtypeStruct((1,) + tall, F32),) * 3,
        in_specs=[vmem] * 3 + [hbm] * 6,
        out_specs=(vmem,) * 3,
        scratch_shapes=[
            pltpu.VMEM(teacher_gate.shape[::-1], BF16),
            pltpu.VMEM(teacher_up.shape[::-1], BF16),
            pltpu.VMEM(teacher_down.shape, BF16),
            pltpu.VMEM((units, width), BF16),
            pltpu.VMEM((units, width), BF16),
            pltpu.VMEM((units, width), BF16),
            pltpu.VMEM(teacher_down.shape[::-1], BF16),
            pltpu.VMEM((width, units), BF16),
            pltpu.VMEM((group, width), BF16),
            pltpu.VMEM((peers, width, tok_count), BF16),
            pltpu.VMEM((peers, experts, tok_count), F32),
            pltpu.VMEM((units, group), F32),
            pltpu.VMEM((units, group), F32),
            pltpu.VMEM((units, group), BF16),
            pltpu.VMEM((units, group), BF16),
            pltpu.VMEM((units, group), BF16),
            pltpu.VMEM((width, group), BF16),
            pltpu.VMEM((line, width, tok_count), F32),
            pltpu.VMEM((line, width, tok_count), BF16),
            pltpu.VMEM((line, width, tok_count), BF16),
            pltpu.VMEM((line, width, tok_count), BF16),
            pltpu.VMEM((line, width, tok_count), BF16),
            pltpu.VMEM((3, PAIR) + tall, BF16),
            pltpu.VMEM((3, PAIR) + tall, BF16),
            pltpu.VMEM((3, PAIR) + tall, F32),
            pltpu.VMEM((PAIR, PAIR) + tall, F32),
            pltpu.VMEM((3,) + tall, BF16),
            pltpu.VMEM((3,) + tall, BF16),
            dma((6,)),
            dma((peers - 1,)),
            dma((peers - 1,)),
            dma((2, peers, PIECES)),
            dma((2, line, PIECES)),
            dma((2, line + 1, PIECES)),
            dma((2, line + 1, Y_FIRST)),
            dma((line, PIECES)),
            dma((line, PIECES)),
            dma((line, PIECES)),
            dma((line, PIECES)),
            dma((3, PAIR)),
            dma((3, PAIR)),
            dma((3,)),
            dma((3,)),
        ],
        compiler_params=pltpu.CompilerParams(
            collective_id=0, has_side_effects=True, vmem_limit_bytes=58 * 1024 * 1024
        ),
        cost_estimate=pl.CostEstimate(
            flops=flops, bytes_accessed=8 * width * units, transcendentals=2 * group * units
        ),
    )(
        tokens,
        router.T,
        expert_lists.T,
        teacher_gate.T,
        teacher_up.T,
        teacher_down,
        jnp.swapaxes(expert_gate, 1, 2),
        jnp.swapaxes(expert_up, 1, 2),
        expert_down,
    )
    return (jnp.swapaxes(grad_gate, 1, 2), jnp.swapaxes(grad_up, 1, 2), grad_down)


def fits_kernel(mesh):
    return mesh.shape["dp"] == PAIR * PAIR and mesh.shape["expert"] <= 4 * PAIR


def solution(mesh):
    return jax.shard_map(
        fused_on_device if fits_kernel(mesh) else on_device,
        mesh=mesh,
        in_specs=(
            P(("dp", "expert"), None),
            P(),
            P(("dp", "expert"), None),
            P(("dp", "expert"), None),
            P(None, "expert"),
            P(None, "expert"),
            P("expert", None),
            P("expert", None, None),
            P("expert", None, None),
            P("expert", None, None),
        ),
        out_specs=(P("expert", "dp", None), P("expert", "dp", None), P("expert", None, "dp")),
        check_vma=False,
    )
```

```python
import functools
import math

import jax
import jax.numpy as jnp
from jax import lax
from jax.experimental import pallas as pl
from jax.experimental.pallas import tpu as pltpu
from jax.sharding import PartitionSpec as P


def silu_value(values):
    return values * jax.nn.sigmoid(values)


def teacher_rows(row_block, teacher_gate, teacher_up, teacher_down):
    pre_a = jnp.dot(row_block, teacher_gate, preferred_element_type=jnp.float32)
    pre_b = jnp.dot(row_block, teacher_up, preferred_element_type=jnp.float32)
    hidden_block = (silu_value(pre_a) * pre_b).astype(jnp.bfloat16)
    return jnp.dot(hidden_block, teacher_down, preferred_element_type=jnp.float32)


def make_term(group_tokens, teacher_gate, teacher_up, teacher_down):

    def teacher_term(first_row, row_count):
        return teacher_rows(group_tokens, teacher_gate, teacher_up, teacher_down)

    return teacher_term


def expert_forward(expert_rows, expert_gate, expert_up, expert_down):
    pre_gate = jnp.dot(expert_rows, expert_gate[0], preferred_element_type=jnp.float32)
    pre_up = jnp.dot(expert_rows, expert_up[0], preferred_element_type=jnp.float32)
    hidden = (silu_value(pre_gate) * pre_up).astype(jnp.bfloat16)
    output = jnp.dot(hidden, expert_down[0], preferred_element_type=jnp.float32).astype(
        jnp.bfloat16
    )
    return (pre_gate, pre_up, hidden, output)


def send_back(output_blocks):
    return lax.all_to_all(output_blocks, "expert", split_axis=0, concat_axis=0, tiled=True)


def on_device(
    tokens,
    router,
    expert_lists,
    slot_positions,
    teacher_gate,
    teacher_up,
    teacher_down,
    expert_gate,
    expert_up,
    expert_down,
):
    tok_count, model_width = tokens.shape
    top_count = expert_lists.shape[1]
    experts = router.shape[1]
    expert_devices = lax.axis_size("expert")
    data_devices = lax.axis_size("dp")
    capacity = 5 * tok_count // experts
    loss_scale = top_count / math.sqrt(
        tok_count * data_devices * expert_devices * top_count / experts
    )
    logits = jnp.dot(tokens.astype(jnp.float32), router, precision=lax.Precision.HIGHEST)
    chosen_mask = expert_lists[:, :, None] == jnp.arange(experts, dtype=jnp.int32)[None, None, :]
    picked = jnp.sum(jnp.where(chosen_mask, logits[:, None, :], 0.0), axis=2)
    sigmoid_pick = jax.nn.sigmoid(picked)
    weights = sigmoid_pick / jnp.sum(sigmoid_pick, axis=1, keepdims=True)
    position = expert_lists * capacity + slot_positions
    entry_index = (
        jnp.zeros((experts * capacity,), jnp.int32)
        .at[position.reshape(-1)]
        .set(jnp.arange(tok_count * top_count, dtype=jnp.int32) + 1)
    )
    filled = entry_index > 0
    entry_row = jnp.maximum(entry_index - 1, 0)
    group_tokens = lax.all_gather(tokens, "expert", axis=0, tiled=True)
    teacher_term = make_term(group_tokens, teacher_gate, teacher_up, teacher_down)
    target = lax.psum_scatter(
        teacher_term(jnp.int32(0), lax.axis_size("expert") * tok_count).astype(jnp.bfloat16),
        "expert",
        scatter_dimension=0,
        tiled=True,
    )
    lists_group, slots_group = (
        lax.all_gather(expert_lists, "expert", axis=0, tiled=True),
        lax.all_gather(slot_positions, "expert", axis=0, tiled=True),
    )
    my_expert = lax.axis_index("expert")
    group_count = lists_group.shape[0]
    source = (jnp.arange(group_count, dtype=jnp.int32) // tok_count)[:, None]
    local_slot = jnp.where(
        lists_group == my_expert, source * capacity + slots_group, expert_devices * capacity
    )
    owner_index = (
        jnp.zeros((expert_devices * capacity,), jnp.int32)
        .at[local_slot.reshape(-1)]
        .set(jnp.repeat(jnp.arange(group_count, dtype=jnp.int32) + 1, top_count), mode="drop")
    )
    expert_rows = jnp.where(
        (owner_index > 0)[:, None],
        group_tokens[jnp.maximum(owner_index - 1, 0)],
        jnp.zeros((), jnp.bfloat16),
    )
    pre_gate, pre_up, hidden, output = expert_forward(
        expert_rows, expert_gate, expert_up, expert_down
    )
    returned = send_back(output.reshape(expert_devices, capacity, model_width))
    flat_back = returned.reshape(experts * capacity, model_width)
    copies = flat_back[position]
    student = jnp.sum(weights[:, :, None] * copies.astype(jnp.float32), axis=1)
    scaled_error = (student - target.astype(jnp.float32)) * loss_scale
    cotangent = (
        (weights[:, :, None] * scaled_error[:, None, :])
        .astype(jnp.bfloat16)
        .reshape(tok_count * top_count, model_width)
    )
    cot_send = jnp.where(
        filled[:, None], cotangent[entry_row], jnp.zeros((), jnp.bfloat16)
    ).reshape(experts, capacity, model_width)
    cot_recv = lax.all_to_all(cot_send, "expert", split_axis=0, concat_axis=0, tiled=True).reshape(
        -1, model_width
    )
    grad_hidden = lax.dot_general(
        cot_recv, expert_down[0], (((1,), (1,)), ((), ())), preferred_element_type=jnp.float32
    )
    gate_sigmoid = jax.nn.sigmoid(pre_gate)
    grad_pre_gate = (
        grad_hidden * pre_up * gate_sigmoid * (1.0 + pre_gate * (1.0 - gate_sigmoid))
    ).astype(jnp.bfloat16)
    grad_pre_up = (grad_hidden * (pre_gate * gate_sigmoid)).astype(jnp.bfloat16)
    part_down = lax.dot_general(
        hidden, cot_recv, (((0,), (0,)), ((), ())), preferred_element_type=jnp.float32
    )
    part_gate = lax.dot_general(
        expert_rows, grad_pre_gate, (((0,), (0,)), ((), ())), preferred_element_type=jnp.float32
    )
    part_up = lax.dot_general(
        expert_rows, grad_pre_up, (((0,), (0,)), ((), ())), preferred_element_type=jnp.float32
    )
    sum_gate, sum_up = (
        lax.psum_scatter(
            part_gate.astype(jnp.bfloat16), "dp", scatter_dimension=0, tiled=True
        ).astype(jnp.float32),
        lax.psum_scatter(
            part_up.astype(jnp.bfloat16), "dp", scatter_dimension=0, tiled=True
        ).astype(jnp.float32),
    )
    sum_down = lax.psum_scatter(
        part_down.astype(jnp.bfloat16), "dp", scatter_dimension=1, tiled=True
    ).astype(jnp.float32)
    return (sum_gate[None], sum_up[None], sum_down[None])


PAIR = 2
PIECES = 4
Y_FIRST = 1
ROW_BY_ROW = (((1,), (1,)), ((), ()))
BF16 = jnp.bfloat16
F32 = jnp.float32


def near_first(count):
    return [sorted(range(count), key=lambda d, z=z: (abs(d - z), d < z if 2 * z < count else d > z)) for z in range(count)]


def fused_kernel(
    line,
    data_devices,
    loss_scale,
    tokens_ref,
    router_ref,
    lists_ref,
    tgate_hbm,
    tup_hbm,
    tdown_hbm,
    gate_hbm,
    up_hbm,
    down_hbm,
    own_out,
    x_recv,
    tgate,
    tup,
    tdown,
    egate,
    eup,
    edown,
    tdown_turned,
    edown_turned,
    rows_buf,
    err_buf,
    w_buf,
    pre_gate,
    pre_up,
    hidden,
    grad_pre_gate,
    grad_pre_up,
    cot,
    part_own,
    y_send,
    y_recv,
    z_send,
    z_recv,
    core_send,
    core_recv,
    keep,
    down_early,
    x_send,
    z_pass,
    own_sem,
    pass_rsem,
    load_sem,
    w_ssem,
    w_rsem,
    ag_rsem,
    ag_ysem,
    ag_zsem,
    ag_osem,
    rs_ysem,
    rs_yrsem,
    rs_zsem,
    rs_zrsem,
    c_ssem,
    c_rsem,
    x_ssem,
    x_rsem,
):
    tok_count, width = tokens_ref.shape
    experts = router_ref.shape[0]
    dp = lax.axis_index("dp")
    me = lax.axis_index("expert")
    z = me // PAIR
    y = me % PAIR
    peers = line * PAIR
    pair_rows = PAIR * tok_count
    y_peer = (dp, me + 1 - 2 * y)
    x_at = dp // PAIR
    core = dp % PAIR
    core_peer = (dp + 1 - 2 * core, me)
    x_peer = (dp + PAIR - 2 * PAIR * x_at, me)
    table = near_first(line)

    def order(step):
        value = jnp.int32(0)
        for at in range(line):
            value = jnp.where(z == at, table[at][step], value)
        return value

    def remote(src, dst, ssem, rsem, device):
        return pltpu.make_async_remote_copy(
            src_ref=src,
            dst_ref=dst,
            send_sem=ssem,
            recv_sem=rsem,
            device_id=device,
            device_id_type=pl.DeviceIdType.MESH,
        )

    barrier = pltpu.get_barrier_semaphore()
    for step in range(1, peers):
        pl.semaphore_signal(
            barrier,
            inc=1,
            device_id=(dp, (me + step) % peers),
            device_id_type=pl.DeviceIdType.MESH,
        )
    for device in (core_peer, x_peer):
        pl.semaphore_signal(
            barrier, inc=1, device_id=device, device_id_type=pl.DeviceIdType.MESH
        )
    loads = [
        pltpu.make_async_copy(src, dst, load_sem.at[at])
        for at, (src, dst) in enumerate(
            (
                (tgate_hbm, tgate),
                (tup_hbm, tup),
                (tdown_hbm, tdown),
                (gate_hbm.at[0], egate),
                (up_hbm.at[0], eup),
                (down_hbm.at[0], edown),
            )
        )
    ]
    for load in loads:
        load.start()

    def piece_of(buf, block, piece):
        if len(buf.shape) == 3:
            span = buf.shape[1] // PIECES
            return buf.at[block, pl.ds(piece * span, span)]
        span = tok_count // PIECES
        first = pl.multiple_of(block * tok_count + piece * span, span)
        return buf.at[pl.ds(first, span)]

    rows_buf[pl.ds(pl.multiple_of(me * tok_count, tok_count), tok_count), :] = tokens_ref[...]
    pl.semaphore_wait(barrier, peers - 1 + 2)

    def own_copies(buf, turn, piece):
        mine = piece_of(buf, me, piece)
        arrival = ag_rsem.at[turn, me, piece]
        sent = ag_zsem.at[turn]
        return (
            remote(mine, mine, ag_ysem.at[turn, z, piece], arrival, y_peer),
            remote(mine, mine, sent.at[z, piece], arrival, (dp, me + PAIR)),
            remote(mine, mine, sent.at[line, piece], arrival, (dp, me - PAIR)),
        )

    def gather_start(buf, turn, piece):
        across, rising, falling = own_copies(buf, turn, piece)

        @pl.when(z < line - 1)
        def _():
            rising.start()

        @pl.when(z > 0)
        def _():
            falling.start()

        across.start()

    def onward_copies(buf, turn, d, piece):
        block = d * PAIR + y
        at = piece_of(buf, block, piece)
        arrival = ag_rsem.at[turn, block, piece]
        device = (dp, jnp.where(d < z, me + PAIR, me - PAIR))
        return (
            remote(at, at, ag_ysem.at[turn, d, piece], arrival, y_peer),
            remote(at, at, ag_zsem.at[turn, d, piece], arrival, device),
            jnp.where(d < z, z < line - 1, z > 0),
        )

    def relay_copies(buf, turn, piece):
        block = me + 1 - 2 * y
        at = piece_of(buf, block, piece)
        arrival = ag_rsem.at[turn, block, piece]
        sent = ag_osem.at[turn]
        return (
            remote(at, at, sent.at[z, piece], arrival, (dp, me + PAIR)),
            remote(at, at, sent.at[line, piece], arrival, (dp, me - PAIR)),
        )

    def other_onward(buf, turn, d, piece):
        block = d * PAIR + 1 - y
        at = piece_of(buf, block, piece)
        device = (dp, jnp.where(d < z, me + PAIR, me - PAIR))
        return (
            remote(at, at, ag_osem.at[turn, d, piece], ag_rsem.at[turn, block, piece], device),
            jnp.where(d < z, z < line - 1, z > 0),
        )

    def gather_rest(buf, turn, work):
        def recv(block, piece):
            at = piece_of(buf, block, piece)
            remote(
                at, at, ag_ysem.at[turn, 0, piece], ag_rsem.at[turn, block, piece], y_peer
            ).wait_recv()

        def do_work(step):
            for piece in range(Y_FIRST, PIECES):
                recv(order(step) * PAIR + 1 - y, piece)
            work(step)

        for piece in range(Y_FIRST):
            recv(me + 1 - 2 * y, piece)
            rising, falling = relay_copies(buf, turn, piece)

            @pl.when(z < line - 1)
            def _():
                rising.start()

            @pl.when(z > 0)
            def _():
                falling.start()

        done = 0
        for step in range(1, line):
            d = order(step)
            for piece in range(PIECES):
                recv(d * PAIR + y, piece)
                across, further, onward = onward_copies(buf, turn, d, piece)

                @pl.when(onward)
                def _():
                    further.start()

                if piece >= Y_FIRST:
                    across.start()
            for piece in range(Y_FIRST):
                recv(d * PAIR + 1 - y, piece)
                beside, onward = other_onward(buf, turn, d, piece)

                @pl.when(onward)
                def _():
                    beside.start()

            if step > 1 or line == 2:
                while done < step:
                    do_work(done)
                    done += 1
        while done < line:
            do_work(done)
            done += 1

    def gather_drain(buf, turn):
        for piece in range(PIECES):
            across, rising, falling = own_copies(buf, turn, piece)

            @pl.when(z < line - 1)
            def _():
                rising.wait_send()

            @pl.when(z > 0)
            def _():
                falling.wait_send()

            across.wait_send()
            for step in range(1, line):
                across, further, onward = onward_copies(buf, turn, order(step), piece)

                @pl.when(onward)
                def _():
                    further.wait_send()

                if piece >= Y_FIRST:
                    across.wait_send()
        for piece in range(Y_FIRST):
            rising, falling = relay_copies(buf, turn, piece)

            @pl.when(z < line - 1)
            def _():
                rising.wait_send()

            @pl.when(z > 0)
            def _():
                falling.wait_send()

            for step in range(1, line):
                beside, onward = other_onward(buf, turn, order(step), piece)

                @pl.when(onward)
                def _():
                    beside.wait_send()


    for piece in range(PIECES):
        gather_start(rows_buf, 0, piece)

    logits = lax.dot_general(
        router_ref[...],
        tokens_ref[...].astype(F32),
        ROW_BY_ROW,
        precision=lax.Precision.HIGHEST,
        preferred_element_type=F32,
    )
    expert_ids = lax.broadcasted_iota(jnp.int32, (experts, tok_count), 0)
    chosen = lists_ref[0:1, :] == expert_ids
    for k in range(1, lists_ref.shape[0]):
        chosen = jnp.logical_or(chosen, lists_ref[k : k + 1, :] == expert_ids)
    picked = jnp.where(chosen, jax.nn.sigmoid(logits), 0.0)
    w_buf[me] = picked / jnp.sum(picked, axis=0, keepdims=True)
    w_copies = []
    for step in range(1, peers):
        copy = remote(
            w_buf.at[me],
            w_buf.at[me],
            w_ssem.at[step - 1],
            w_rsem.at[step - 1],
            (dp, (me + step) % peers),
        )
        copy.start()
        w_copies.append(copy)
    for load in loads:
        load.wait()
    edown_turned[...] = edown[...].T
    tdown_turned[...] = tdown[...].T
    for copy in w_copies:
        copy.wait()

    def pair_weights(d):
        return jnp.concatenate(
            [w_buf[d * PAIR + part, pl.ds(me, 1), :] for part in range(PAIR)], axis=1
        )

    def place_of(step):
        return pl.ds(step * pair_rows, pair_rows)

    def pair_of(d):
        return pl.ds(pl.multiple_of(d * pair_rows, pair_rows), pair_rows)

    span = width // PIECES

    def y_copy(d, piece):
        at = (d, pl.ds(piece * span, span))
        return remote(
            y_send.at[at],
            y_recv.at[at],
            rs_ysem.at[d, piece],
            rs_yrsem.at[d, piece],
            y_peer,
        )

    def z_copy(d, piece):
        part_rows = pl.ds(piece * span, span)
        return remote(
            z_send.at[d, part_rows],
            z_recv.at[z, part_rows],
            rs_zsem.at[d, piece],
            rs_zrsem.at[z, piece],
            (dp, d * PAIR + y),
        )

    passing = line >= 4
    at_end = jnp.logical_or(z == 0, z == line - 1)

    def pass_copy(d, piece):
        rising = d > z
        way = jnp.where(rising, 0, 1)
        part_rows = pl.ds(piece * span, span)
        return remote(
            z_send.at[d, part_rows],
            z_pass.at[way, part_rows],
            rs_zsem.at[d, piece],
            pass_rsem.at[way, piece],
            (dp, jnp.where(rising, me + PAIR, me - PAIR)),
        )

    def forward(step):
        d = order(step)
        where = place_of(step)
        rows = rows_buf[pair_of(d), :]

        def product(table):
            return lax.dot_general(table[...], rows, ROW_BY_ROW, preferred_element_type=F32)

        gate_values = product(egate)
        up_values = product(eup)
        pre_gate[:, where] = gate_values
        pre_up[:, where] = up_values
        hidden_values = (silu_value(gate_values) * up_values).astype(BF16)
        hidden[:, where] = hidden_values
        teacher_hidden = (silu_value(product(tgate)) * product(tup)).astype(BF16)
        scale = pair_weights(d)
        for piece in range(PIECES):
            at = pl.ds(piece * span, span)
            output = jnp.dot(edown_turned[at, :], hidden_values, preferred_element_type=F32)
            teacher = jnp.dot(tdown_turned[at, :], teacher_hidden, preferred_element_type=F32)
            partial = scale * output - teacher
            low = partial[:, :tok_count]
            high = partial[:, tok_count:]
            y_send[d, at] = jnp.where(y == 0, high, low).astype(BF16)
            y_copy(d, piece).start()
            part_own[d, at] = jnp.where(y == 0, low, high)
        if step > 1:
            for piece in range(PIECES):
                combine(step - 1, piece)

    def combine(step, piece):
        d = order(step)
        at = pl.ds(piece * span, span)
        y_copy(d, piece).wait_recv()
        total = part_own[d, at] + y_recv[d, at].astype(F32)
        if step == 0:
            part_own[d, at] = total
        elif step < line - 1 or not passing:
            z_send[d, at] = total.astype(BF16)
            z_copy(d, piece).start()
        else:
            handed = jnp.logical_or(z == 1, z == line - 2)

            @pl.when(at_end)
            def _():
                z_send[d, at] = total.astype(BF16)
                pass_copy(d, piece).start()

            @pl.when(handed)
            def _():
                pass_copy(d, piece).wait_recv()
                way = jnp.where(d > z, 0, 1)
                z_send[d, at] = (total + z_pass[way, at].astype(F32)).astype(BF16)
                z_copy(d, piece).start()

            @pl.when(jnp.logical_not(jnp.logical_or(at_end, handed)))
            def _():
                z_send[d, at] = total.astype(BF16)
                z_copy(d, piece).start()

    gather_rest(rows_buf, 0, forward)
    for piece in range(PIECES):
        combine(line - 1, piece)
    for piece in range(PIECES):
        combine(0, piece)
    for piece in range(PIECES):
        at = pl.ds(piece * span, span)
        for step in range(1, line):
            source = order(step)

            def take():
                remote(
                    z_send.at[source, at],
                    z_recv.at[source, at],
                    rs_zsem.at[source, piece],
                    rs_zrsem.at[source, piece],
                    y_peer,
                ).wait_recv()
                part_own[z, at] += z_recv[source, at].astype(F32)

            if step == line - 1 and passing:
                pl.when(jnp.logical_not(at_end))(take)
            else:
                take()
        err_buf[me, at] = (part_own[z, at] * loss_scale).astype(BF16)
        gather_start(err_buf, 1, piece)

    gather_drain(rows_buf, 0)
    for piece in range(PIECES):
        for step in range(line):
            d = order(step)
            y_copy(d, piece).wait_send()
            if step:
                z_copy(d, piece).wait_send()

    quarter = width // data_devices
    x_of = (1 - x_at, x_at)
    early = (line - 1) * pair_rows

    def columns_of(q):
        return pl.ds(pl.multiple_of(q * quarter, quarter), quarter)

    def cotangents(step):
        d = order(step)
        errors = jnp.concatenate([err_buf[d * PAIR + part] for part in range(PAIR)], axis=1)
        cot[:, place_of(step)] = (pair_weights(d) * errors.astype(F32)).astype(BF16)

    def hidden_grads(step):
        where = place_of(step)
        grad_hidden = jnp.dot(edown[...], cot[:, where], preferred_element_type=F32)
        gate_values = pre_gate[:, where]
        gate_sigmoid = jax.nn.sigmoid(gate_values)
        there = pair_of(order(step))
        grad_pre_gate[:, there] = (
            grad_hidden
            * pre_up[:, where]
            * gate_sigmoid
            * (1.0 + gate_values * (1.0 - gate_sigmoid))
        ).astype(BF16)
        grad_pre_up[:, there] = (grad_hidden * (gate_values * gate_sigmoid)).astype(BF16)

    def down_part(q, first, count):
        span_of = pl.ds(first, count)
        return lax.dot_general(
            hidden[:, span_of],
            cot[columns_of(q), span_of],
            ROW_BY_ROW,
            preferred_element_type=F32,
        )

    def backward(step):
        cotangents(step)
        if step < line - 1:
            hidden_grads(step)
        if step == line - 2:
            for slot in range(PAIR):
                for side in range(PAIR):
                    down_early[slot, side] = down_part(x_of[slot] * PAIR + side, 0, early)

    gather_rest(err_buf, 1, backward)

    def part(which, slot, side):
        q = x_of[slot] * PAIR + side
        if which == 2:
            return down_early[slot, side] + down_part(q, early, pair_rows)
        grads = grad_pre_gate if which == 0 else grad_pre_up
        return jnp.dot(grads[...], rows_buf[:, columns_of(q)], preferred_element_type=F32)

    def core_copy(which, slot):
        return remote(
            core_send.at[which, slot],
            core_recv.at[which, slot],
            c_ssem.at[which, slot],
            c_rsem.at[which, slot],
            core_peer,
        )

    def x_copy(which):
        return remote(
            x_send.at[which],
            x_recv.at[which],
            x_ssem.at[which],
            x_rsem.at[which],
            x_peer,
        )

    def own_copy(which):
        return pltpu.make_async_copy(keep.at[which, 1], own_out.at[which], own_sem.at[which])

    def join(which, slot):
        core_copy(which, slot).wait_recv()
        total = keep[which, slot] + core_recv[which, slot].astype(F32)
        if slot == 0:
            x_send[which] = total.astype(BF16)
            x_copy(which).start()
        else:
            keep[which, slot] = total
            own_copy(which).start()

    items = [(which, slot) for slot in range(PAIR) for which in (2, 0, 1)]
    for at, (which, slot) in enumerate(items):
        core_send[which, slot] = part(which, slot, 1 - core).astype(BF16)
        core_copy(which, slot).start()
        keep[which, slot] = part(which, slot, core)
        if at == 0:
            hidden_grads(line - 1)
            join(which, slot)
        elif at > 1:
            join(*items[at - 1])
    join(*items[-1])
    gather_drain(err_buf, 1)
    for which in range(3):
        own_copy(which).wait()
        x_copy(which).wait()
        for slot in range(PAIR):
            core_copy(which, slot).wait_send()


def fused_on_device(
    tokens,
    router,
    expert_lists,
    slot_positions,
    teacher_gate,
    teacher_up,
    teacher_down,
    expert_gate,
    expert_up,
    expert_down,
):
    tok_count, width = tokens.shape
    experts = router.shape[1]
    top_count = expert_lists.shape[1]
    peers = lax.axis_size("expert")
    data_devices = lax.axis_size("dp")
    line = peers // PAIR
    units = expert_gate.shape[2]
    group = peers * tok_count
    quarter = width // data_devices
    loss_scale = top_count / math.sqrt(group * data_devices * top_count / experts)
    vmem = pl.BlockSpec(memory_space=pltpu.VMEM)
    hbm = pl.BlockSpec(memory_space=pl.ANY)
    flops = 2 * group * width * (3 * teacher_gate.shape[1] + 7 * units)
    tall = (units, quarter)
    dma = pltpu.SemaphoreType.DMA
    own, arrived = pl.pallas_call(
        functools.partial(fused_kernel, line, data_devices, loss_scale),
        out_shape=(
            jax.ShapeDtypeStruct((3,) + tall, F32),
            jax.ShapeDtypeStruct((3,) + tall, BF16),
        ),
        in_specs=[vmem] * 3 + [hbm] * 6,
        out_specs=(hbm,) * 2,
        scratch_shapes=[
            pltpu.VMEM(teacher_gate.shape[::-1], BF16),
            pltpu.VMEM(teacher_up.shape[::-1], BF16),
            pltpu.VMEM(teacher_down.shape, BF16),
            pltpu.VMEM((units, width), BF16),
            pltpu.VMEM((units, width), BF16),
            pltpu.VMEM((units, width), BF16),
            pltpu.VMEM(teacher_down.shape[::-1], BF16),
            pltpu.VMEM((width, units), BF16),
            pltpu.VMEM((group, width), BF16),
            pltpu.VMEM((peers, width, tok_count), BF16),
            pltpu.VMEM((peers, experts, tok_count), F32),
            pltpu.VMEM((units, group), F32),
            pltpu.VMEM((units, group), F32),
            pltpu.VMEM((units, group), BF16),
            pltpu.VMEM((units, group), BF16),
            pltpu.VMEM((units, group), BF16),
            pltpu.VMEM((width, group), BF16),
            pltpu.VMEM((line, width, tok_count), F32),
            pltpu.VMEM((line, width, tok_count), BF16),
            pltpu.VMEM((line, width, tok_count), BF16),
            pltpu.VMEM((line, width, tok_count), BF16),
            pltpu.VMEM((line, width, tok_count), BF16),
            pltpu.VMEM((3, PAIR) + tall, BF16),
            pltpu.VMEM((3, PAIR) + tall, BF16),
            pltpu.VMEM((3, PAIR) + tall, F32),
            pltpu.VMEM((PAIR, PAIR) + tall, F32),
            pltpu.VMEM((3,) + tall, BF16),
            pltpu.VMEM((2, width, tok_count), BF16),
            dma((3,)),
            dma((2, PIECES)),
            dma((6,)),
            dma((peers - 1,)),
            dma((peers - 1,)),
            dma((2, peers, PIECES)),
            dma((2, line, PIECES)),
            dma((2, line + 1, PIECES)),
            dma((2, line + 1, Y_FIRST)),
            dma((line, PIECES)),
            dma((line, PIECES)),
            dma((line, PIECES)),
            dma((line, PIECES)),
            dma((3, PAIR)),
            dma((3, PAIR)),
            dma((3,)),
            dma((3,)),
        ],
        compiler_params=pltpu.CompilerParams(
            collective_id=0, has_side_effects=True, vmem_limit_bytes=58 * 1024 * 1024
        ),
        cost_estimate=pl.CostEstimate(
            flops=flops, bytes_accessed=8 * width * units, transcendentals=2 * group * units
        ),
    )(
        tokens,
        router.T,
        expert_lists.T,
        teacher_gate.T,
        teacher_up.T,
        teacher_down,
        jnp.swapaxes(expert_gate, 1, 2),
        jnp.swapaxes(expert_up, 1, 2),
        expert_down,
    )
    grads = [own[at : at + 1] + arrived[at : at + 1].astype(F32) for at in range(3)]
    return (jnp.swapaxes(grads[0], 1, 2), jnp.swapaxes(grads[1], 1, 2), grads[2])


def fits_kernel(mesh):
    return mesh.shape["dp"] == PAIR * PAIR and mesh.shape["expert"] <= 4 * PAIR


def solution(mesh):
    return jax.shard_map(
        fused_on_device if fits_kernel(mesh) else on_device,
        mesh=mesh,
        in_specs=(
            P(("dp", "expert"), None),
            P(),
            P(("dp", "expert"), None),
            P(("dp", "expert"), None),
            P(None, "expert"),
            P(None, "expert"),
            P("expert", None),
            P("expert", None, None),
            P("expert", None, None),
            P("expert", None, None),
        ),
        out_specs=(P("expert", "dp", None), P("expert", "dp", None), P("expert", None, "dp")),
        check_vma=False,
    )
```

```python
import functools
import math

import jax
import jax.numpy as jnp
from jax import lax
from jax.experimental import pallas as pl
from jax.experimental.pallas import tpu as pltpu
from jax.sharding import PartitionSpec as P


def silu_value(values):
    return values * jax.nn.sigmoid(values)


def teacher_rows(row_block, teacher_gate, teacher_up, teacher_down):
    pre_a = jnp.dot(row_block, teacher_gate, preferred_element_type=jnp.float32)
    pre_b = jnp.dot(row_block, teacher_up, preferred_element_type=jnp.float32)
    hidden_block = (silu_value(pre_a) * pre_b).astype(jnp.bfloat16)
    return jnp.dot(hidden_block, teacher_down, preferred_element_type=jnp.float32)


def make_term(group_tokens, teacher_gate, teacher_up, teacher_down):

    def teacher_term(first_row, row_count):
        return teacher_rows(group_tokens, teacher_gate, teacher_up, teacher_down)

    return teacher_term


def expert_forward(expert_rows, expert_gate, expert_up, expert_down):
    pre_gate = jnp.dot(expert_rows, expert_gate[0], preferred_element_type=jnp.float32)
    pre_up = jnp.dot(expert_rows, expert_up[0], preferred_element_type=jnp.float32)
    hidden = (silu_value(pre_gate) * pre_up).astype(jnp.bfloat16)
    output = jnp.dot(hidden, expert_down[0], preferred_element_type=jnp.float32).astype(
        jnp.bfloat16
    )
    return (pre_gate, pre_up, hidden, output)


def send_back(output_blocks):
    return lax.all_to_all(output_blocks, "expert", split_axis=0, concat_axis=0, tiled=True)


def on_device(
    tokens,
    router,
    expert_lists,
    slot_positions,
    teacher_gate,
    teacher_up,
    teacher_down,
    expert_gate,
    expert_up,
    expert_down,
):
    tok_count, model_width = tokens.shape
    top_count = expert_lists.shape[1]
    experts = router.shape[1]
    expert_devices = lax.axis_size("expert")
    data_devices = lax.axis_size("dp")
    capacity = 5 * tok_count // experts
    loss_scale = top_count / math.sqrt(
        tok_count * data_devices * expert_devices * top_count / experts
    )
    logits = jnp.dot(tokens.astype(jnp.float32), router, precision=lax.Precision.HIGHEST)
    chosen_mask = expert_lists[:, :, None] == jnp.arange(experts, dtype=jnp.int32)[None, None, :]
    picked = jnp.sum(jnp.where(chosen_mask, logits[:, None, :], 0.0), axis=2)
    sigmoid_pick = jax.nn.sigmoid(picked)
    weights = sigmoid_pick / jnp.sum(sigmoid_pick, axis=1, keepdims=True)
    position = expert_lists * capacity + slot_positions
    entry_index = (
        jnp.zeros((experts * capacity,), jnp.int32)
        .at[position.reshape(-1)]
        .set(jnp.arange(tok_count * top_count, dtype=jnp.int32) + 1)
    )
    filled = entry_index > 0
    entry_row = jnp.maximum(entry_index - 1, 0)
    group_tokens = lax.all_gather(tokens, "expert", axis=0, tiled=True)
    teacher_term = make_term(group_tokens, teacher_gate, teacher_up, teacher_down)
    target = lax.psum_scatter(
        teacher_term(jnp.int32(0), lax.axis_size("expert") * tok_count).astype(jnp.bfloat16),
        "expert",
        scatter_dimension=0,
        tiled=True,
    )
    lists_group, slots_group = (
        lax.all_gather(expert_lists, "expert", axis=0, tiled=True),
        lax.all_gather(slot_positions, "expert", axis=0, tiled=True),
    )
    my_expert = lax.axis_index("expert")
    group_count = lists_group.shape[0]
    source = (jnp.arange(group_count, dtype=jnp.int32) // tok_count)[:, None]
    local_slot = jnp.where(
        lists_group == my_expert, source * capacity + slots_group, expert_devices * capacity
    )
    owner_index = (
        jnp.zeros((expert_devices * capacity,), jnp.int32)
        .at[local_slot.reshape(-1)]
        .set(jnp.repeat(jnp.arange(group_count, dtype=jnp.int32) + 1, top_count), mode="drop")
    )
    expert_rows = jnp.where(
        (owner_index > 0)[:, None],
        group_tokens[jnp.maximum(owner_index - 1, 0)],
        jnp.zeros((), jnp.bfloat16),
    )
    pre_gate, pre_up, hidden, output = expert_forward(
        expert_rows, expert_gate, expert_up, expert_down
    )
    returned = send_back(output.reshape(expert_devices, capacity, model_width))
    flat_back = returned.reshape(experts * capacity, model_width)
    copies = flat_back[position]
    student = jnp.sum(weights[:, :, None] * copies.astype(jnp.float32), axis=1)
    scaled_error = (student - target.astype(jnp.float32)) * loss_scale
    cotangent = (
        (weights[:, :, None] * scaled_error[:, None, :])
        .astype(jnp.bfloat16)
        .reshape(tok_count * top_count, model_width)
    )
    cot_send = jnp.where(
        filled[:, None], cotangent[entry_row], jnp.zeros((), jnp.bfloat16)
    ).reshape(experts, capacity, model_width)
    cot_recv = lax.all_to_all(cot_send, "expert", split_axis=0, concat_axis=0, tiled=True).reshape(
        -1, model_width
    )
    grad_hidden = lax.dot_general(
        cot_recv, expert_down[0], (((1,), (1,)), ((), ())), preferred_element_type=jnp.float32
    )
    gate_sigmoid = jax.nn.sigmoid(pre_gate)
    grad_pre_gate = (
        grad_hidden * pre_up * gate_sigmoid * (1.0 + pre_gate * (1.0 - gate_sigmoid))
    ).astype(jnp.bfloat16)
    grad_pre_up = (grad_hidden * (pre_gate * gate_sigmoid)).astype(jnp.bfloat16)
    part_down = lax.dot_general(
        hidden, cot_recv, (((0,), (0,)), ((), ())), preferred_element_type=jnp.float32
    )
    part_gate = lax.dot_general(
        expert_rows, grad_pre_gate, (((0,), (0,)), ((), ())), preferred_element_type=jnp.float32
    )
    part_up = lax.dot_general(
        expert_rows, grad_pre_up, (((0,), (0,)), ((), ())), preferred_element_type=jnp.float32
    )
    sum_gate, sum_up = (
        lax.psum_scatter(
            part_gate.astype(jnp.bfloat16), "dp", scatter_dimension=0, tiled=True
        ).astype(jnp.float32),
        lax.psum_scatter(
            part_up.astype(jnp.bfloat16), "dp", scatter_dimension=0, tiled=True
        ).astype(jnp.float32),
    )
    sum_down = lax.psum_scatter(
        part_down.astype(jnp.bfloat16), "dp", scatter_dimension=1, tiled=True
    ).astype(jnp.float32)
    return (sum_gate[None], sum_up[None], sum_down[None])


PAIR = 2
PIECES = 8
Y_FIRST = 2
ROW_BY_ROW = (((1,), (1,)), ((), ()))
BF16 = jnp.bfloat16
F32 = jnp.float32


def near_first(count):
    return [sorted(range(count), key=lambda d, z=z: (abs(d - z), d < z if 2 * z < count else d > z)) for z in range(count)]


def fused_kernel(
    line,
    data_devices,
    loss_scale,
    tokens_ref,
    router_ref,
    lists_ref,
    tgate_hbm,
    tup_hbm,
    tdown_hbm,
    gate_hbm,
    up_hbm,
    down_hbm,
    own_out,
    x_recv,
    tgate,
    tup,
    tdown,
    egate,
    eup,
    edown,
    tdown_turned,
    edown_turned,
    rows_buf,
    err_buf,
    w_buf,
    pre_gate,
    pre_up,
    hidden,
    grad_pre_gate,
    grad_pre_up,
    cot,
    part_own,
    y_send,
    y_recv,
    z_send,
    z_recv,
    core_send,
    core_recv,
    keep,
    down_early,
    x_send,
    z_pass,
    own_sem,
    pass_rsem,
    load_sem,
    w_ssem,
    w_rsem,
    ag_rsem,
    ag_ysem,
    ag_zsem,
    ag_osem,
    rs_ysem,
    rs_yrsem,
    rs_zsem,
    rs_zrsem,
    c_ssem,
    c_rsem,
    x_ssem,
    x_rsem,
):
    tok_count, width = tokens_ref.shape
    experts = router_ref.shape[0]
    dp = lax.axis_index("dp")
    me = lax.axis_index("expert")
    z = me // PAIR
    y = me % PAIR
    peers = line * PAIR
    pair_rows = PAIR * tok_count
    y_peer = (dp, me + 1 - 2 * y)
    x_at = dp // PAIR
    core = dp % PAIR
    core_peer = (dp + 1 - 2 * core, me)
    x_peer = (dp + PAIR - 2 * PAIR * x_at, me)
    table = near_first(line)

    def order(step):
        value = jnp.int32(0)
        for at in range(line):
            value = jnp.where(z == at, table[at][step], value)
        return value

    def remote(src, dst, ssem, rsem, device):
        return pltpu.make_async_remote_copy(
            src_ref=src,
            dst_ref=dst,
            send_sem=ssem,
            recv_sem=rsem,
            device_id=device,
            device_id_type=pl.DeviceIdType.MESH,
        )

    barrier = pltpu.get_barrier_semaphore()
    for step in range(1, peers):
        pl.semaphore_signal(
            barrier,
            inc=1,
            device_id=(dp, (me + step) % peers),
            device_id_type=pl.DeviceIdType.MESH,
        )
    for device in (core_peer, x_peer):
        pl.semaphore_signal(
            barrier, inc=1, device_id=device, device_id_type=pl.DeviceIdType.MESH
        )
    loads = [
        pltpu.make_async_copy(src, dst, load_sem.at[at])
        for at, (src, dst) in enumerate(
            (
                (tgate_hbm, tgate),
                (tup_hbm, tup),
                (tdown_hbm, tdown),
                (gate_hbm.at[0], egate),
                (up_hbm.at[0], eup),
                (down_hbm.at[0], edown),
            )
        )
    ]
    for load in loads:
        load.start()

    def piece_of(buf, block, piece):
        if len(buf.shape) == 3:
            span = buf.shape[1] // PIECES
            return buf.at[block, pl.ds(piece * span, span)]
        span = tok_count // PIECES
        first = pl.multiple_of(block * tok_count + piece * span, span)
        return buf.at[pl.ds(first, span)]

    rows_buf[pl.ds(pl.multiple_of(me * tok_count, tok_count), tok_count), :] = tokens_ref[...]
    pl.semaphore_wait(barrier, peers - 1 + 2)

    def own_copies(buf, turn, piece):
        mine = piece_of(buf, me, piece)
        arrival = ag_rsem.at[turn, me, piece]
        sent = ag_zsem.at[turn]
        return (
            remote(mine, mine, ag_ysem.at[turn, z, piece], arrival, y_peer),
            remote(mine, mine, sent.at[z, piece], arrival, (dp, me + PAIR)),
            remote(mine, mine, sent.at[line, piece], arrival, (dp, me - PAIR)),
        )

    def gather_start(buf, turn, piece):
        across, rising, falling = own_copies(buf, turn, piece)

        @pl.when(z < line - 1)
        def _():
            rising.start()

        @pl.when(z > 0)
        def _():
            falling.start()

        across.start()

    def onward_copies(buf, turn, d, piece):
        block = d * PAIR + y
        at = piece_of(buf, block, piece)
        arrival = ag_rsem.at[turn, block, piece]
        device = (dp, jnp.where(d < z, me + PAIR, me - PAIR))
        return (
            remote(at, at, ag_ysem.at[turn, d, piece], arrival, y_peer),
            remote(at, at, ag_zsem.at[turn, d, piece], arrival, device),
            jnp.where(d < z, z < line - 1, z > 0),
        )

    def relay_copies(buf, turn, piece):
        block = me + 1 - 2 * y
        at = piece_of(buf, block, piece)
        arrival = ag_rsem.at[turn, block, piece]
        sent = ag_osem.at[turn]
        return (
            remote(at, at, sent.at[z, piece], arrival, (dp, me + PAIR)),
            remote(at, at, sent.at[line, piece], arrival, (dp, me - PAIR)),
        )

    def other_onward(buf, turn, d, piece):
        block = d * PAIR + 1 - y
        at = piece_of(buf, block, piece)
        device = (dp, jnp.where(d < z, me + PAIR, me - PAIR))
        return (
            remote(at, at, ag_osem.at[turn, d, piece], ag_rsem.at[turn, block, piece], device),
            jnp.where(d < z, z < line - 1, z > 0),
        )

    def gather_rest(buf, turn, work):
        def recv(block, piece):
            at = piece_of(buf, block, piece)
            remote(
                at, at, ag_ysem.at[turn, 0, piece], ag_rsem.at[turn, block, piece], y_peer
            ).wait_recv()

        def do_work(step):
            for piece in range(Y_FIRST, PIECES):
                recv(order(step) * PAIR + 1 - y, piece)
            work(step)

        for piece in range(Y_FIRST):
            recv(me + 1 - 2 * y, piece)
            rising, falling = relay_copies(buf, turn, piece)

            @pl.when(z < line - 1)
            def _():
                rising.start()

            @pl.when(z > 0)
            def _():
                falling.start()

        done = 0
        for step in range(1, line):
            d = order(step)
            for piece in range(PIECES):
                recv(d * PAIR + y, piece)
                across, further, onward = onward_copies(buf, turn, d, piece)

                @pl.when(onward)
                def _():
                    further.start()

                if piece >= Y_FIRST:
                    across.start()
            for piece in range(Y_FIRST):
                recv(d * PAIR + 1 - y, piece)
                beside, onward = other_onward(buf, turn, d, piece)

                @pl.when(onward)
                def _():
                    beside.start()

            if step > 1 or line == 2:
                while done < step:
                    do_work(done)
                    done += 1
        while done < line:
            do_work(done)
            done += 1

    def gather_drain(buf, turn):
        for piece in range(PIECES):
            across, rising, falling = own_copies(buf, turn, piece)

            @pl.when(z < line - 1)
            def _():
                rising.wait_send()

            @pl.when(z > 0)
            def _():
                falling.wait_send()

            across.wait_send()
            for step in range(1, line):
                across, further, onward = onward_copies(buf, turn, order(step), piece)

                @pl.when(onward)
                def _():
                    further.wait_send()

                if piece >= Y_FIRST:
                    across.wait_send()
        for piece in range(Y_FIRST):
            rising, falling = relay_copies(buf, turn, piece)

            @pl.when(z < line - 1)
            def _():
                rising.wait_send()

            @pl.when(z > 0)
            def _():
                falling.wait_send()

            for step in range(1, line):
                beside, onward = other_onward(buf, turn, order(step), piece)

                @pl.when(onward)
                def _():
                    beside.wait_send()


    for piece in range(PIECES):
        gather_start(rows_buf, 0, piece)

    logits = lax.dot_general(
        router_ref[...],
        tokens_ref[...].astype(F32),
        ROW_BY_ROW,
        precision=lax.Precision.HIGHEST,
        preferred_element_type=F32,
    )
    expert_ids = lax.broadcasted_iota(jnp.int32, (experts, tok_count), 0)
    chosen = lists_ref[0:1, :] == expert_ids
    for k in range(1, lists_ref.shape[0]):
        chosen = jnp.logical_or(chosen, lists_ref[k : k + 1, :] == expert_ids)
    picked = jnp.where(chosen, jax.nn.sigmoid(logits), 0.0)
    w_buf[me] = picked / jnp.sum(picked, axis=0, keepdims=True)
    w_copies = []
    for step in range(1, peers):
        copy = remote(
            w_buf.at[me],
            w_buf.at[me],
            w_ssem.at[step - 1],
            w_rsem.at[step - 1],
            (dp, (me + step) % peers),
        )
        copy.start()
        w_copies.append(copy)
    for load in loads:
        load.wait()
    edown_turned[...] = edown[...].T
    tdown_turned[...] = tdown[...].T
    for copy in w_copies:
        copy.wait()

    def pair_weights(d):
        return jnp.concatenate(
            [w_buf[d * PAIR + part, pl.ds(me, 1), :] for part in range(PAIR)], axis=1
        )

    def place_of(step):
        return pl.ds(step * pair_rows, pair_rows)

    def pair_of(d):
        return pl.ds(pl.multiple_of(d * pair_rows, pair_rows), pair_rows)

    span = width // PIECES

    def y_copy(d, piece):
        at = (d, pl.ds(piece * span, span))
        return remote(
            y_send.at[at],
            y_recv.at[at],
            rs_ysem.at[d, piece],
            rs_yrsem.at[d, piece],
            y_peer,
        )

    def z_copy(d, piece):
        part_rows = pl.ds(piece * span, span)
        return remote(
            z_send.at[d, part_rows],
            z_recv.at[z, part_rows],
            rs_zsem.at[d, piece],
            rs_zrsem.at[z, piece],
            (dp, d * PAIR + y),
        )

    passing = line >= 4
    at_end = jnp.logical_or(z == 0, z == line - 1)

    def pass_copy(d, piece):
        rising = d > z
        way = jnp.where(rising, 0, 1)
        part_rows = pl.ds(piece * span, span)
        return remote(
            z_send.at[d, part_rows],
            z_pass.at[way, part_rows],
            rs_zsem.at[d, piece],
            pass_rsem.at[way, piece],
            (dp, jnp.where(rising, me + PAIR, me - PAIR)),
        )

    def forward(step):
        d = order(step)
        where = place_of(step)
        rows = rows_buf[pair_of(d), :]

        def product(table):
            return lax.dot_general(table[...], rows, ROW_BY_ROW, preferred_element_type=F32)

        gate_values = product(egate)
        up_values = product(eup)
        pre_gate[:, where] = gate_values
        pre_up[:, where] = up_values
        hidden_values = (silu_value(gate_values) * up_values).astype(BF16)
        hidden[:, where] = hidden_values
        teacher_hidden = (silu_value(product(tgate)) * product(tup)).astype(BF16)
        scale = pair_weights(d)
        for piece in range(PIECES):
            at = pl.ds(piece * span, span)
            output = jnp.dot(edown_turned[at, :], hidden_values, preferred_element_type=F32)
            teacher = jnp.dot(tdown_turned[at, :], teacher_hidden, preferred_element_type=F32)
            partial = scale * output - teacher
            low = partial[:, :tok_count]
            high = partial[:, tok_count:]
            y_send[d, at] = jnp.where(y == 0, high, low).astype(BF16)
            y_copy(d, piece).start()
            part_own[d, at] = jnp.where(y == 0, low, high)
        if step > 1:
            for piece in range(PIECES):
                combine(step - 1, piece)

    def combine(step, piece):
        d = order(step)
        at = pl.ds(piece * span, span)
        y_copy(d, piece).wait_recv()
        total = part_own[d, at] + y_recv[d, at].astype(F32)
        if step == 0:
            part_own[d, at] = total
        elif step < line - 1 or not passing:
            z_send[d, at] = total.astype(BF16)
            z_copy(d, piece).start()
        else:
            handed = jnp.logical_or(z == 1, z == line - 2)

            @pl.when(at_end)
            def _():
                z_send[d, at] = total.astype(BF16)
                pass_copy(d, piece).start()

            @pl.when(handed)
            def _():
                pass_copy(d, piece).wait_recv()
                way = jnp.where(d > z, 0, 1)
                z_send[d, at] = (total + z_pass[way, at].astype(F32)).astype(BF16)
                z_copy(d, piece).start()

            @pl.when(jnp.logical_not(jnp.logical_or(at_end, handed)))
            def _():
                z_send[d, at] = total.astype(BF16)
                z_copy(d, piece).start()

    gather_rest(rows_buf, 0, forward)
    for piece in range(PIECES):
        combine(line - 1, piece)
    for piece in range(PIECES):
        combine(0, piece)
    for piece in range(PIECES):
        at = pl.ds(piece * span, span)
        for step in range(1, line):
            source = order(step)

            def take():
                remote(
                    z_send.at[source, at],
                    z_recv.at[source, at],
                    rs_zsem.at[source, piece],
                    rs_zrsem.at[source, piece],
                    y_peer,
                ).wait_recv()
                part_own[z, at] += z_recv[source, at].astype(F32)

            if step == line - 1 and passing:
                pl.when(jnp.logical_not(at_end))(take)
            else:
                take()
        err_buf[me, at] = (part_own[z, at] * loss_scale).astype(BF16)
        gather_start(err_buf, 1, piece)

    gather_drain(rows_buf, 0)
    for piece in range(PIECES):
        for step in range(line):
            d = order(step)
            y_copy(d, piece).wait_send()
            if step:
                z_copy(d, piece).wait_send()

    quarter = width // data_devices
    x_of = (1 - x_at, x_at)
    early = (line - 1) * pair_rows

    def columns_of(q):
        return pl.ds(pl.multiple_of(q * quarter, quarter), quarter)

    def cotangents(step):
        d = order(step)
        errors = jnp.concatenate([err_buf[d * PAIR + part] for part in range(PAIR)], axis=1)
        cot[:, place_of(step)] = (pair_weights(d) * errors.astype(F32)).astype(BF16)

    def hidden_grads(step):
        where = place_of(step)
        grad_hidden = jnp.dot(edown[...], cot[:, where], preferred_element_type=F32)
        gate_values = pre_gate[:, where]
        gate_sigmoid = jax.nn.sigmoid(gate_values)
        there = pair_of(order(step))
        grad_pre_gate[:, there] = (
            grad_hidden
            * pre_up[:, where]
            * gate_sigmoid
            * (1.0 + gate_values * (1.0 - gate_sigmoid))
        ).astype(BF16)
        grad_pre_up[:, there] = (grad_hidden * (gate_values * gate_sigmoid)).astype(BF16)

    def down_part(q, first, count):
        span_of = pl.ds(first, count)
        return lax.dot_general(
            hidden[:, span_of],
            cot[columns_of(q), span_of],
            ROW_BY_ROW,
            preferred_element_type=F32,
        )

    def backward(step):
        cotangents(step)
        if step < line - 1:
            hidden_grads(step)
        if step == line - 2:
            for slot in range(PAIR):
                for side in range(PAIR):
                    down_early[slot, side] = down_part(x_of[slot] * PAIR + side, 0, early)

    gather_rest(err_buf, 1, backward)

    def part(which, slot, side):
        q = x_of[slot] * PAIR + side
        if which == 2:
            return down_early[slot, side] + down_part(q, early, pair_rows)
        grads = grad_pre_gate if which == 0 else grad_pre_up
        return jnp.dot(grads[...], rows_buf[:, columns_of(q)], preferred_element_type=F32)

    def core_copy(which, slot):
        return remote(
            core_send.at[which, slot],
            core_recv.at[which, slot],
            c_ssem.at[which, slot],
            c_rsem.at[which, slot],
            core_peer,
        )

    def x_copy(which):
        return remote(
            x_send.at[which],
            x_recv.at[which],
            x_ssem.at[which],
            x_rsem.at[which],
            x_peer,
        )

    def own_copy(which):
        return pltpu.make_async_copy(keep.at[which, 1], own_out.at[which], own_sem.at[which])

    def join(which, slot):
        core_copy(which, slot).wait_recv()
        total = keep[which, slot] + core_recv[which, slot].astype(F32)
        if slot == 0:
            x_send[which] = total.astype(BF16)
            x_copy(which).start()
        else:
            keep[which, slot] = total
            own_copy(which).start()

    items = [(which, slot) for slot in range(PAIR) for which in (2, 0, 1)]
    for at, (which, slot) in enumerate(items):
        core_send[which, slot] = part(which, slot, 1 - core).astype(BF16)
        core_copy(which, slot).start()
        keep[which, slot] = part(which, slot, core)
        if at == 0:
            hidden_grads(line - 1)
            join(which, slot)
        elif at > 1:
            join(*items[at - 1])
    join(*items[-1])
    gather_drain(err_buf, 1)
    for which in range(3):
        own_copy(which).wait()
        x_copy(which).wait()
        for slot in range(PAIR):
            core_copy(which, slot).wait_send()


def fused_on_device(
    tokens,
    router,
    expert_lists,
    slot_positions,
    teacher_gate,
    teacher_up,
    teacher_down,
    expert_gate,
    expert_up,
    expert_down,
):
    tok_count, width = tokens.shape
    experts = router.shape[1]
    top_count = expert_lists.shape[1]
    peers = lax.axis_size("expert")
    data_devices = lax.axis_size("dp")
    line = peers // PAIR
    units = expert_gate.shape[2]
    group = peers * tok_count
    quarter = width // data_devices
    loss_scale = top_count / math.sqrt(group * data_devices * top_count / experts)
    vmem = pl.BlockSpec(memory_space=pltpu.VMEM)
    hbm = pl.BlockSpec(memory_space=pl.ANY)
    flops = 2 * group * width * (3 * teacher_gate.shape[1] + 7 * units)
    tall = (units, quarter)
    dma = pltpu.SemaphoreType.DMA
    own, arrived = pl.pallas_call(
        functools.partial(fused_kernel, line, data_devices, loss_scale),
        out_shape=(
            jax.ShapeDtypeStruct((3,) + tall, F32),
            jax.ShapeDtypeStruct((3,) + tall, BF16),
        ),
        in_specs=[vmem] * 3 + [hbm] * 6,
        out_specs=(hbm,) * 2,
        scratch_shapes=[
            pltpu.VMEM(teacher_gate.shape[::-1], BF16),
            pltpu.VMEM(teacher_up.shape[::-1], BF16),
            pltpu.VMEM(teacher_down.shape, BF16),
            pltpu.VMEM((units, width), BF16),
            pltpu.VMEM((units, width), BF16),
            pltpu.VMEM((units, width), BF16),
            pltpu.VMEM(teacher_down.shape[::-1], BF16),
            pltpu.VMEM((width, units), BF16),
            pltpu.VMEM((group, width), BF16),
            pltpu.VMEM((peers, width, tok_count), BF16),
            pltpu.VMEM((peers, experts, tok_count), F32),
            pltpu.VMEM((units, group), F32),
            pltpu.VMEM((units, group), F32),
            pltpu.VMEM((units, group), BF16),
            pltpu.VMEM((units, group), BF16),
            pltpu.VMEM((units, group), BF16),
            pltpu.VMEM((width, group), BF16),
            pltpu.VMEM((line, width, tok_count), F32),
            pltpu.VMEM((line, width, tok_count), BF16),
            pltpu.VMEM((line, width, tok_count), BF16),
            pltpu.VMEM((line, width, tok_count), BF16),
            pltpu.VMEM((line, width, tok_count), BF16),
            pltpu.VMEM((3, PAIR) + tall, BF16),
            pltpu.VMEM((3, PAIR) + tall, BF16),
            pltpu.VMEM((3, PAIR) + tall, F32),
            pltpu.VMEM((PAIR, PAIR) + tall, F32),
            pltpu.VMEM((3,) + tall, BF16),
            pltpu.VMEM((2, width, tok_count), BF16),
            dma((3,)),
            dma((2, PIECES)),
            dma((6,)),
            dma((peers - 1,)),
            dma((peers - 1,)),
            dma((2, peers, PIECES)),
            dma((2, line, PIECES)),
            dma((2, line + 1, PIECES)),
            dma((2, line + 1, Y_FIRST)),
            dma((line, PIECES)),
            dma((line, PIECES)),
            dma((line, PIECES)),
            dma((line, PIECES)),
            dma((3, PAIR)),
            dma((3, PAIR)),
            dma((3,)),
            dma((3,)),
        ],
        compiler_params=pltpu.CompilerParams(
            collective_id=0, has_side_effects=True, vmem_limit_bytes=58 * 1024 * 1024
        ),
        cost_estimate=pl.CostEstimate(
            flops=flops, bytes_accessed=8 * width * units, transcendentals=2 * group * units
        ),
    )(
        tokens,
        router.T,
        expert_lists.T,
        teacher_gate.T,
        teacher_up.T,
        teacher_down,
        jnp.swapaxes(expert_gate, 1, 2),
        jnp.swapaxes(expert_up, 1, 2),
        expert_down,
    )
    grads = [own[at : at + 1] + arrived[at : at + 1].astype(F32) for at in range(3)]
    return (jnp.swapaxes(grads[0], 1, 2), jnp.swapaxes(grads[1], 1, 2), grads[2])


def fits_kernel(mesh):
    return mesh.shape["dp"] == PAIR * PAIR and mesh.shape["expert"] <= 4 * PAIR


def solution(mesh):
    return jax.shard_map(
        fused_on_device if fits_kernel(mesh) else on_device,
        mesh=mesh,
        in_specs=(
            P(("dp", "expert"), None),
            P(),
            P(("dp", "expert"), None),
            P(("dp", "expert"), None),
            P(None, "expert"),
            P(None, "expert"),
            P("expert", None),
            P("expert", None, None),
            P("expert", None, None),
            P("expert", None, None),
        ),
        out_specs=(P("expert", "dp", None), P("expert", "dp", None), P("expert", None, "dp")),
        check_vma=False,
    )
```
